256 devices in a mesh: tm: 32 (over y, z_lo, core), seq: 8 (over x, z_hi).
Axes of the slice: x: 4, y: 4, z: 8 (z_hi: 2, z_lo: 4; z = z_hi * 4 + z_lo), core: 2. Of those that a mesh axis runs over, the one named last changes fastest.
Arguments:
- states: float32 [32, 512, 1536], P('tm', 'seq'), may hold values from -6 to 6
- qkv_weight: bfloat16 [1536, 3, 1536], P('tm', None, 'seq'), may hold values from -0.15625 to 0.15625
- text_kv: bfloat16 [32, 320, 2, 1536], P('tm', 'seq'), may hold values from -180 to 180
- mod_table: float32 [128, 3, 1536], replicated, may hold values from -3 to 3
- step_table: float32 [128], replicated, may hold values from 0.02 to 0.1
- step_ids: int32 [32], P('tm'), may hold values from 0 to 127, as said below
Outputs:
- latents: float32 [32, 512, 1536], P('tm', 'seq')
- changes: float32 [2, 32], P(None, 'tm')
The draws below stay inside these ranges and needn't reach their ends.
Inputs may be any that keep to these rules, and one draw needn't show every extreme that they name: `step_ids`: distinct and strictly decreasing; the first is 127 and the last 0.
All inputs are finite; a program needn't handle non-finite values.
Results may differ from the reference program's by a relative error of at most 0.0017.
The reference program's roundings to bfloat16 on the way (of `modulated`, `projected`, `attn_weights` and `attended`) count: a program that leaves them out, or rounds other values in their place, can miss the bound.
Values may be sent and summed in bfloat16 or wider, within the bound.
No kernel may reach another device: no remote copies, remote signals or barrier semaphores. Data moves between devices by JAX's collectives and lax.ppermute only.
A program may use at most 128 MiB of HBM per device.

```python
import math
import jax
import jax.numpy as jnp
from jax import lax

D = 1536
HEADS = 24
HEAD_DIM = 64
NSCHED = 128
SWEEPS = 2
STEPS = 32
IMG = 512
TXT = 320


def draw_text_kv(key, part):
    key = jax.random.fold_in(key, 11)
    shape = (STEPS, TXT, 2, D)
    return jnp.clip(jax.random.normal(key, shape, jnp.float32), -6.0, 6.0).astype(jnp.bfloat16)


def draw_step_ids(key, part):
    key = jax.random.fold_in(key, 5)
    shuffled = jax.random.permutation(key, NSCHED - 2) + 1
    middle = -jnp.sort(-shuffled[:STEPS - 2])
    ends_high = jnp.full((1,), NSCHED - 1, jnp.int32)
    ends_low = jnp.zeros((1,), jnp.int32)
    return jnp.concatenate([ends_high, middle.astype(jnp.int32), ends_low]).astype(jnp.int32)


def shard_levels(rng, dims, cuts, smallest, largest):
    def one(position, blocks):
        steps = jax.random.uniform(jax.random.fold_in(jax.random.fold_in(rng, 6), position), (blocks,), jnp.float32, smallest / len(cuts), largest / len(cuts))
        return jnp.repeat(jnp.exp(steps), dims[position] // blocks).reshape((-1,) + (1,) * (len(dims) - position - 1))

    level = one(*cuts[0])
    for cut in cuts[1:]:
        level = level * one(*cut)
    return level


def bell_draw(own_key, extent, deviation, reach, cuts=(), kind=jnp.bfloat16):
    gain = shard_levels(own_key, extent, cuts, -0.22, 0.18) if cuts else 1.0
    drawn = jax.random.normal(own_key, extent, jnp.float32) * deviation * gain
    return jnp.minimum(jnp.maximum(drawn, -reach), reach).astype(kind)


def setup_inputs(seed: int = 0) -> dict:
    key_of = jax.random.split(jax.random.key(seed), 7)
    return {
        "states": bell_draw(key_of[0], (STEPS, IMG, D), 1.0, 6.0, ((0, 32), (1, 8)), jnp.float32),
        "qkv_weight": bell_draw(key_of[1], (D, 3, D), D ** -0.5, 0.15625, ((0, 32), (2, 8))),
        "text_kv": draw_text_kv(jax.random.fold_in(key_of[6], 71), 0),
        "mod_table": bell_draw(key_of[3], (NSCHED, 3, D), 0.5, 3.0, (), jnp.float32),
        "step_table": jnp.clip(jnp.exp(jax.random.uniform(key_of[4], (NSCHED,), jnp.float32, math.log(0.02), math.log(0.1))), 0.02, 0.1),
        "step_ids": draw_step_ids(jax.random.fold_in(key_of[6], 71), 0),
    }


def modulate(latent, modulation):
    average = lax.optimization_barrier(jnp.mean(latent, axis=-1, keepdims=True))
    centred = latent - average
    variance = lax.optimization_barrier(jnp.mean(centred * centred, axis=-1, keepdims=True))
    normed = centred * lax.rsqrt(variance + 1e-06)
    return (normed * (1.0 + modulation[1]) + modulation[0]).astype(jnp.bfloat16)

def attend_head(packed):
    query, key_rows, value_rows = packed
    scores = jnp.dot(query, key_rows.T, preferred_element_type=jnp.float32) * HEAD_DIM ** (-0.5)
    top = lax.optimization_barrier(jnp.max(scores, axis=-1, keepdims=True))
    exp_scores = jnp.exp(scores - top)
    attn_weights = (exp_scores / lax.optimization_barrier(jnp.sum(exp_scores, axis=-1, keepdims=True))).astype(jnp.bfloat16)
    return jnp.dot(attn_weights, value_rows, preferred_element_type=jnp.float32).astype(jnp.bfloat16)

def drift_term(latent, weight, text_pair, modulation, step_size):
    modulated = modulate(latent, modulation)
    projected = jnp.dot(modulated, weight.reshape(D, 3 * D), preferred_element_type=jnp.float32).astype(jnp.bfloat16)
    projected = projected.reshape(IMG, 3, HEADS, HEAD_DIM)
    queries = projected[:, 0]
    key_rows = jnp.concatenate([projected[:, 1], text_pair[:, 0].reshape(TXT, HEADS, HEAD_DIM)], axis=0)
    value_rows = jnp.concatenate([projected[:, 2], text_pair[:, 1].reshape(TXT, HEADS, HEAD_DIM)], axis=0)
    attended = lax.map(attend_head, (queries.transpose(1, 0, 2), key_rows.transpose(1, 0, 2), value_rows.transpose(1, 0, 2)))
    attended = attended.transpose(1, 0, 2).reshape(IMG, D).astype(jnp.float32)
    return step_size * (latent + modulation[2] * attended)

def reference(states, qkv_weight, text_kv, mod_table, step_table, step_ids):
    step_sizes = -step_table[step_ids]
    modulations = mod_table[step_ids]
    changes = []
    latents = states

    def one_step(packed):
        return drift_term(packed[0], qkv_weight, packed[1], packed[2], packed[3])
    for sweep_index in range(SWEEPS):
        terms = lax.map(one_step, (latents, text_kv, modulations, step_sizes))
        terms = terms.at[0].add(latents[0])
        totals = jnp.cumsum(terms, axis=0)
        updated = jnp.concatenate([latents[:1], totals[:-1]], axis=0)
        changes.append(lax.optimization_barrier(jnp.max(jnp.abs(updated - latents), axis=(1, 2))))
        latents = updated
    return (latents, jnp.stack(changes))
```

```python
import functools
import itertools

import jax
import jax.numpy as jnp
from jax import lax
from jax.experimental import pallas as pl
from jax.experimental.pallas import tpu as pltpu
from jax.sharding import Mesh, PartitionSpec as P

AXES = ("y", "zl", "c", "x", "zh")
SIZES = {"y": 4, "zl": 4, "c": 2, "x": 4, "zh": 2}

HEAD_DIM = 64
SWEEPS = 2
D = 1536
HALF = 768
HW = 192
ROWS = 64
TOK = 512
TXT = 320
KEYS = TOK + TXT
VMEM_LIMIT = 48 * 1024 * 1024
f32, bf16 = jnp.float32, jnp.bfloat16


def permute(value, axes, move):
    def index(place):
        flat = 0
        for name in axes:
            flat = flat * SIZES[name] + place[name] % SIZES[name]
        return flat

    pairs = []
    for coords in itertools.product(*[range(SIZES[name]) for name in axes]):
        place = dict(zip(axes, coords))
        target = move(dict(place))
        if target is not None:
            pairs.append((index(place), index(target)))
    return lax.ppermute(value, axes if len(axes) > 1 else axes[0], pairs)


def shift(value, axis, amount):
    return permute(value, (axis,), lambda p: {axis: p[axis] + amount})


def forward(value, axis, amount):
    return permute(
        value, (axis,),
        lambda p: {axis: p[axis] + amount} if p[axis] + amount < SIZES[axis] else None,
    )


def shift_z(value, amount):
    def move(p):
        ring = (p["zh"] * 4 + p["zl"] + amount) % 8
        return {"zl": ring % 4, "zh": ring // 4}

    return permute(value, ("zl", "zh"), move)


def swap_core_zh(value, same):
    moved = permute(
        value, ("c", "zh"),
        lambda p: None if p["c"] == p["zh"] else {"c": p["zh"], "zh": p["c"]},
    )
    return jnp.where(same, value, moved)


def call(kernel, out_shape, n_vmem, n_smem, flops=0, nbytes=0, scratch=()):
    return pl.pallas_call(
        kernel,
        out_shape=out_shape,
        in_specs=[pl.BlockSpec(memory_space=pltpu.SMEM)] * n_smem
        + [pl.BlockSpec(memory_space=pltpu.VMEM)] * n_vmem,
        out_specs=jax.tree.map(lambda _: pl.BlockSpec(memory_space=pltpu.VMEM), out_shape),
        scratch_shapes=list(scratch),
        compiler_params=pltpu.CompilerParams(vmem_limit_bytes=VMEM_LIMIT),
        cost_estimate=pl.CostEstimate(flops=flops, bytes_accessed=nbytes, transcendentals=0),
    )


def struct(*shape, dtype=f32):
    return jax.ShapeDtypeStruct(shape, dtype)


def first_norm_kernel(lat_ref, mod_ref, out_ref, send_ref):
    latent = lat_ref[...]
    average = jnp.mean(latent, axis=-1, keepdims=True)
    centred = latent - average
    variance = jnp.mean(centred * centred, axis=-1, keepdims=True)
    normed = centred * lax.rsqrt(variance + 1e-06)
    modulated = (normed * (1.0 + mod_ref[1:2, :]) + mod_ref[0:1, :]).astype(bf16)
    for half in range(2):
        cols = [slice(k * 2 * HW + half * HW, k * 2 * HW + (half + 1) * HW) for k in range(4)]
        out_ref[:, half * HALF:(half + 1) * HALF] = jnp.concatenate(
            [modulated[:, s] for s in cols], axis=1
        )
        piece = jnp.concatenate([latent[:, s] for s in cols], axis=1)
        for sub in range(4):
            send_ref[sub * 2 + half] = piece[sub * 16:(sub + 1) * 16]


def weight_kernel(place_ref, *refs):
    pieces, out_ref = refs[:4], refs[4]
    y, zl = place_ref[0], place_ref[1]
    for ky in range(4):
        from_y = lax.rem(y - ky + 4, 4)
        for kz in range(4):
            from_zl = lax.rem(zl - kz + 4, 4)
            row = (from_zl // 2) * HALF + from_y * HW + lax.rem(from_zl, 2) * 96
            out_ref[pl.ds(pl.multiple_of(row, 32), 96), :] = pieces[ky][kz]


def attention_kernel(first, place_ref, *refs):
    blocks = refs[:8]
    w_ref, tk_ref, tv_ref, out_ref, k01, v01, k2, v2, q01, q2 = refs[8:]
    core, x = place_ref[2], place_ref[3]
    if first:
        rows = jnp.concatenate([b[...] for b in blocks], axis=0)
        qkv = jnp.dot(rows, w_ref[...], preferred_element_type=f32)
    else:
        mine = jnp.concatenate([b[...] for b in blocks[:4]], axis=0)
        other = jnp.concatenate([b[...] for b in blocks[4:]], axis=0)
        w_mine = w_ref[pl.ds(pl.multiple_of(core * HALF, HALF), HALF), :]
        w_other = w_ref[pl.ds(pl.multiple_of((1 - core) * HALF, HALF), HALF), :]
        qkv = jnp.dot(mine, w_mine, preferred_element_type=f32)
        qkv = qkv + jnp.dot(other, w_other, preferred_element_type=f32)
    scale = HEAD_DIM ** (-0.5)
    q01[...] = (qkv[:, 0:128] * scale).astype(bf16)
    k01[0:TOK, :] = qkv[:, 128:256].astype(bf16)
    v01[0:TOK, :] = qkv[:, 256:384].astype(bf16)
    q2[...] = (qkv[:, 384:448] * scale).astype(bf16)
    k2[0:TOK, :] = qkv[:, 448:512].astype(bf16)
    v2[0:TOK, :] = qkv[:, 512:576].astype(bf16)
    k01[TOK:, :] = tk_ref[:, 0:128]
    v01[TOK:, :] = tv_ref[:, 0:128]
    k2[TOK:, :] = tk_ref[:, 128:192]
    v2[TOK:, :] = tv_ref[:, 128:192]
    lane = lax.broadcasted_iota(jnp.int32, (128, 128), 1)

    def attend(query, keys, values):
        scores = lax.dot_general(
            query, keys, (((1,), (1,)), ((), ())), preferred_element_type=f32
        )
        top = jnp.max(scores, axis=-1, keepdims=True)
        exp_scores = jnp.exp(scores - top)
        total = jnp.sum(exp_scores, axis=-1, keepdims=True)
        weights = (exp_scores * (1.0 / total)).astype(bf16)
        return jnp.dot(weights, values, preferred_element_type=f32)

    for chunk in range(4):
        span = slice(chunk * 128, (chunk + 1) * 128)
        pair = q01[span, :]
        zero = jnp.zeros_like(pair)
        out0 = attend(jnp.where(lane < 64, pair, zero), k01[...], v01[...])
        out1 = attend(jnp.where(lane < 64, zero, pair), k01[...], v01[...])
        out01 = jnp.where(lane < 64, out0, out1).astype(bf16)
        out2 = attend(q2[span, :], k2[...], v2[...]).astype(bf16)
        from_x = lax.rem(x - (chunk if not first else chunk) + 4, 4)
        for part in range(8):
            if first:
                sub = part % 4
                zh = core if part < 4 else 1 - core
            else:
                sub, zh = part // 2, part % 2
            target = (sub * 4 + from_x) * 2 + zh
            out_ref[target, :, 0:128] = out01[part * 16:(part + 1) * 16]
            out_ref[target, :, 128:HW] = out2[part * 16:(part + 1) * 16]


def terms_kernel(first_ref, dt_ref, att_ref, lat_ref, gate_ref, part_ref, total_ref):
    run = lat_ref[0] * first_ref[0]
    for j in range(8):
        part_ref[j] = run
        sub, zh = j // 2, j % 2
        attended = jnp.concatenate(
            [att_ref[(sub * 4 + k) * 2 + zh].astype(f32) for k in range(4)], axis=1
        )
        run = run + dt_ref[j] * (lat_ref[j] + gate_ref[j:j + 1, :] * attended)
    total_ref[...] = run


def update_kernel(with_stats, part_ref, lat_ref, t1_ref, t2_ref, t3_ref, new_ref, chg_ref,
                  *stats_ref):
    offset = t1_ref[...] + t2_ref[...] + t3_ref[...]
    lane = lax.broadcasted_iota(jnp.int32, (16, 128), 1)
    for j in range(8):
        new = part_ref[j] + offset
        new_ref[j] = new
        change = jnp.max(jnp.abs(new - lat_ref[j]))
        chg_ref[j:j + 1, :] = jnp.full((1, 128), change, f32)
        if with_stats:
            average = jnp.mean(new, axis=-1, keepdims=True)
            centred = new - average
            spread = jnp.sum(centred * centred, axis=-1, keepdims=True)
            stats_ref[0][j] = jnp.where(lane == 0, average, spread)


def modulate_kernel(new_ref, mine_ref, other_ref, shift_ref, scale_ref, out_ref):
    for j in range(8):
        mean_a, mean_b = mine_ref[j][:, 0:1], other_ref[j][:, 0:1]
        spread = mine_ref[j][:, 1:2] + other_ref[j][:, 1:2]
        average = (mean_a + mean_b) * 0.5
        gap = mean_a - mean_b
        variance = (spread + gap * gap * (HALF * 0.5)) * (1.0 / D)
        normed = (new_ref[j] - average) * lax.rsqrt(variance + 1e-06)
        out_ref[j] = (
            normed * (1.0 + scale_ref[j:j + 1, :]) + shift_ref[j:j + 1, :]
        ).astype(bf16)


def place_kernel(in_ref, out_ref):
    for sub in range(4):
        for k in range(4):
            cols = slice(k * HW, (k + 1) * HW)
            out_ref[sub * 16:(sub + 1) * 16, k * 2 * HW:(k + 1) * 2 * HW] = jnp.concatenate(
                [in_ref[sub * 2][:, cols], in_ref[sub * 2 + 1][:, cols]], axis=1
            )


def on_device(states, qkv_weight, text_kv, mod_table, step_table, step_ids):
    y, zl, c, x, zh = (lax.axis_index(name) for name in AXES)
    same = c == zh
    place = jnp.stack([y, zl, c, x]).astype(jnp.int32)
    latent = states[0]

    with jax.named_scope("norm_first"):
        mod_own = lax.dynamic_index_in_dim(mod_table, step_ids[0], 0, keepdims=False)
        modulated, state_send = call(
            first_norm_kernel, (struct(ROWS, D, dtype=bf16), struct(8, 16, HALF)), 2, 0
        )(latent, mod_own)
    with jax.named_scope("gather_first"):
        modulated = swap_core_zh(modulated, same)
        mine = [modulated] + [shift(modulated, "x", k) for k in (1, 2, 3)]
        other = [shift(b, "c", 1) for b in mine]
        blocks = [b for pair in zip(mine, other) for b in pair]

    with jax.named_scope("weights"):
        w = qkv_weight
        w = jnp.concatenate(
            [w[:, 0, :128], w[:, 1, :128], w[:, 2, :128],
             w[:, 0, 128:], w[:, 1, 128:], w[:, 2, 128:]], axis=1
        )
        w_a = permute(w, ("c", "zh"), lambda p: None if p["c"] == p["zh"] else
                      {"c": 1 - p["c"], "zh": p["zh"]})
        w_b = [permute(w, ("c", "zh"), lambda p, k=k: {"c": p["zh"], "zh": 1 - p["zh"]}
                       if p["c"] == k else None) for k in range(2)]
        w0 = jnp.where(same, jnp.where(c == 0, w, w_a), w_b[0])
        w1 = jnp.where(same, jnp.where(c == 1, w, w_a), w_b[1])
        w2 = jnp.concatenate([w0, w1], axis=0)
        w8 = jnp.stack([w2, shift_z(w2, 1), shift_z(w2, 2), shift_z(w2, -1)])
        pieces = [w8] + [shift(w8, "y", k) for k in (1, 2, 3)]
        weight = call(weight_kernel, struct(D, 3 * HW, dtype=bf16), 4, 1)(place, *pieces)

    with jax.named_scope("text"):
        text = text_kv[0].reshape(40, 2, 8, HW).transpose(2, 1, 0, 3)
        text = lax.all_to_all(text, ("x", "zh"), 0, 0)
        text = swap_core_zh(text, same)
        text = text.transpose(1, 0, 2, 3).reshape(2, TXT, HW)

    with jax.named_scope("plan"):
        step_id = step_ids[0].reshape(1, 1)
        mate = shift(step_id, "c", 1)
        pair = jnp.where(c == 0, jnp.concatenate([step_id, mate], 1),
                         jnp.concatenate([mate, step_id], 1))
        pairs = jnp.concatenate([pair] + [shift(pair, "zl", k) for k in (1, 2, 3)], axis=0)
        ids = jnp.take(pairs, lax.rem(zl - jnp.arange(4) + 4, 4), axis=0).reshape(8)
        mods = jnp.take(mod_table, ids, axis=0).reshape(8, 3, 4, 2, HW)
        mods = lax.dynamic_index_in_dim(mods, c, 3, keepdims=False).reshape(8, 3, HALF)
        shifts, scales, gates = mods[:, 0], mods[:, 1], mods[:, 2]
        dts = -jnp.take(step_table, ids)
        is_first = (y == 0).astype(f32).reshape(1)

    with jax.named_scope("states"):
        lat = lax.all_to_all(state_send, ("zl", "c"), 0, 0)

    changes = []
    for sweep in range(SWEEPS):
        last = sweep == SWEEPS - 1
        with jax.named_scope("attention"):
            attended = call(
                functools.partial(attention_kernel, sweep == 0),
                struct(32, 16, HW, dtype=bf16), 11, 1,
                flops=2 * TOK * D * 3 * HW + 4 * TOK * KEYS * HW, nbytes=4 << 20,
                scratch=[
                    pltpu.VMEM((KEYS, 128), bf16), pltpu.VMEM((KEYS, 128), bf16),
                    pltpu.VMEM((KEYS, 64), bf16), pltpu.VMEM((KEYS, 64), bf16),
                    pltpu.VMEM((TOK, 128), bf16), pltpu.VMEM((TOK, 64), bf16),
                ],
            )(place, *blocks, weight, text[0], text[1])
        with jax.named_scope("to_prefix"):
            attended = lax.all_to_all(attended, ("zl", "x", "zh"), 0, 0)
        with jax.named_scope("prefix"):
            part, total = call(
                terms_kernel, (struct(8, 16, HALF), struct(16, HALF)), 3, 2
            )(is_first, dts, attended, lat, gates)
            earlier = [forward(total, "y", k) for k in (1, 2, 3)]
            outs = (struct(8, 16, HALF), struct(8, 128))
            if not last:
                outs = outs + (struct(8, 16, 128),)
            new, change, *stats = call(
                functools.partial(update_kernel, not last), outs, 5, 0
            )(part, lat, *earlier)
        changes.append(change)
        lat = new
        if not last:
            with jax.named_scope("norm"):
                stats = stats[0]
                modulated = call(
                    modulate_kernel, struct(8, 16, HALF, dtype=bf16), 5, 0
                )(new, stats, shift(stats, "c", 1), shifts, scales)
            with jax.named_scope("gather"):
                modulated = lax.all_to_all(modulated, ("zl", "zh"), 0, 0).reshape(128, HALF)
                mine = [modulated] + [shift(modulated, "x", k) for k in (1, 2, 3)]
                blocks = mine + [shift(b, "c", 1) for b in mine]
    with jax.named_scope("place"):
        out = lax.all_to_all(lat, ("zl", "c"), 0, 0)
        out = call(place_kernel, struct(ROWS, D), 1, 0)(out)
    with jax.named_scope("changes"):
        top = jnp.concatenate(changes, axis=0)
        top = jnp.maximum(top, shift(top, "c", 1))
        top = functools.reduce(jnp.maximum, [top] + [shift(top, "x", k) for k in (1, 2, 3)])
        for amount in (1, 2):
            top = jnp.maximum(top, permute(top, ("zl",), lambda p: {"zl": p["zl"] ^ amount}))
        top = jnp.maximum(top, shift(top, "zh", 1))
        top = top[:, 0].reshape(SWEEPS, 8)
        top = lax.dynamic_slice_in_dim(top, zl * 2 + c, 1, axis=1)
    return out[None], top


def solution(mesh):
    fine = Mesh(mesh.devices.reshape([SIZES[name] for name in AXES]), AXES)
    tm, seq = ("y", "zl", "c"), ("x", "zh")
    in_specs = (
        P(tm, seq, None), P(tm, None, seq), P(tm, seq, None, None), P(), P(), P(tm),
    )
    out_specs = (P(tm, seq, None), P(None, tm))
    return jax.shard_map(
        on_device, mesh=fine, in_specs=in_specs, out_specs=out_specs, check_vma=False
    )
```

```python
import functools
import itertools

import jax
import jax.numpy as jnp
from jax import lax
from jax.experimental import pallas as pl
from jax.experimental.pallas import tpu as pltpu
from jax.sharding import Mesh, PartitionSpec as P

AXES = ("y", "zl", "c", "x", "zh")
SIZES = {"y": 4, "zl": 4, "c": 2, "x": 4, "zh": 2}

HEAD_DIM = 64
SWEEPS = 2
D = 1536
HALF = 768
BLOCK = 384
HW = 192
ROWS = 64
TOK = 512
TXT = 320
KEYS = TOK + TXT
MIB = 1024 * 1024
f32, bf16 = jnp.float32, jnp.bfloat16


def permute(value, axes, move):
    def index(place):
        flat = 0
        for name in axes:
            flat = flat * SIZES[name] + place[name] % SIZES[name]
        return flat

    pairs = []
    for coords in itertools.product(*[range(SIZES[name]) for name in axes]):
        place = dict(zip(axes, coords))
        target = move(dict(place))
        if target is not None:
            pairs.append((index(place), index(target)))
    return lax.ppermute(value, axes if len(axes) > 1 else axes[0], pairs)


def shift(value, axis, amount):
    return permute(value, (axis,), lambda p: {axis: p[axis] + amount})


def shift_z(value, amount):
    def move(p):
        ring = (p["zh"] * 4 + p["zl"] + amount) % 8
        return {"zl": ring % 4, "zh": ring // 4}

    return permute(value, ("zl", "zh"), move)


def swap_core_zh(value, same):
    moved = permute(
        value, ("c", "zh"),
        lambda p: None if p["c"] == p["zh"] else {"c": p["zh"], "zh": p["c"]},
    )
    return jnp.where(same, value, moved)


def call(kernel, out_shape, n_vmem, n_smem, limit=6, after=0):
    return pl.pallas_call(
        kernel,
        out_shape=out_shape,
        in_specs=[pl.BlockSpec(memory_space=pltpu.SMEM)] * n_smem
        + [pl.BlockSpec(memory_space=pltpu.VMEM)] * n_vmem
        + [pl.BlockSpec(memory_space=pl.ANY)] * after,
        out_specs=jax.tree.map(lambda _: pl.BlockSpec(memory_space=pltpu.VMEM), out_shape),
        compiler_params=pltpu.CompilerParams(vmem_limit_bytes=limit * MIB),
    )


def struct(*shape, dtype=f32):
    return jax.ShapeDtypeStruct(shape, dtype)


def half_columns(half):
    return [slice(k * 2 * HW + half * HW, k * 2 * HW + (half + 1) * HW) for k in range(4)]


def columns_kernel(w_ref, after_ref, out_ref):
    raw = w_ref[...].astype(f32)
    parts = [raw[:, k, :128] for k in range(3)] + [raw[:, k, 128:] for k in range(3)]
    out_ref[...] = jnp.concatenate(parts, axis=1).astype(bf16)


def start_kernel(place_ref, ids_ref, steps_ref, lat_ref, mod_ref, text_ref,
                 out_ref, keep_ref, mate_ref):
    latent = lat_ref[0]
    average = jnp.mean(latent, axis=-1, keepdims=True)
    centred = latent - average
    variance = jnp.mean(centred * centred, axis=-1, keepdims=True)
    normed = centred * lax.rsqrt(variance + 1e-06)
    modulated = (normed * (1.0 + mod_ref[1:2, :]) + mod_ref[0:1, :]).astype(bf16)
    raw = text_ref[0].astype(f32)
    rows = jnp.concatenate([raw[:, 0, :], raw[:, 1, :]], axis=0).astype(bf16)
    step = jnp.full((5, HALF), -steps_ref[ids_ref[0]], f32)
    for half in range(2):
        piece = jnp.concatenate([modulated[:, s] for s in half_columns(half)], axis=1)
        out_ref[half * 2, 0:64] = piece[:, 0:BLOCK]
        out_ref[half * 2 + 1, 0:64] = piece[:, BLOCK:]
        piece = jnp.concatenate([latent[:, s] for s in half_columns(half)], axis=1)
        mods = jnp.concatenate([mod_ref[:, s] for s in half_columns(half)], axis=1)
        below = jnp.concatenate([mods, step], axis=0)
        for ref, wanted in ((keep_ref, place_ref[2]), (mate_ref, 1 - place_ref[2])):
            @pl.when(wanted == half)
            def _(ref=ref, piece=piece, below=below):
                for sub in range(4):
                    ref[sub, 0:16] = piece[sub * 16:(sub + 1) * 16]
                    ref[sub, 16:24] = below
    for k in range(4):
        out_ref[k, 64:144] = rows[:, k * BLOCK:(k + 1) * BLOCK]


def hold_kernel(in_ref, *refs):
    refs[-1][...] = in_ref[...]


def message_kernel(place_ref, keep_ref, mate_ref, after_ref, *out_refs):
    zl, core = place_ref[1], place_ref[2]
    for k in range(4):
        target = lax.rem(zl + k, 4)
        out_refs[k][core] = keep_ref[target]
        out_refs[k][1 - core] = mate_ref[target]


def send_kernel(place_ref, in_ref, *out_refs):
    x = place_ref[3]
    for k in range(4):
        for block in range(4):
            out_refs[k][block * 64:(block + 1) * 64] = in_ref[block, 0:64]
        out_refs[k][256:336] = in_ref[lax.rem(x + k, 4), 64:144]


def weight_rows(place_ref):
    y, zl = place_ref[0], place_ref[1]
    for ky in range(4):
        from_y = lax.rem(y - ky + 4, 4)
        for kz in range(4):
            from_zl = lax.rem(zl - kz + 4, 4)
            row = (from_zl // 2) * HALF + from_y * HW + lax.rem(from_zl, 2) * 96
            yield ky, kz, pl.ds(pl.multiple_of(row, 32), 96)


def weight_piece(pieces, ky, kz):
    own, after, far_a, far_b, last = pieces
    if ky == 2:
        return (far_a if kz < 2 else far_b).at[kz % 2]
    return (own, after, None, last)[ky].at[kz]


def weight_kernel(place_ref, *refs):
    for ky, kz, rows in weight_rows(place_ref):
        refs[-1][rows, :] = weight_piece(refs[:5], ky, kz)[...]


def attention_kernel(first, place_ref, *refs):
    blocks, refs = refs[:8], refs[8:]
    if first:
        w_ref, out_ref, keep_ref, k01, v01, k2, v2, q01, q2 = refs
    else:
        w_ref, text_ref, out_ref, k01, v01, k2, v2, q01, q2 = refs
    core, x = place_ref[2], place_ref[3]
    if first:
        rows = jnp.concatenate([
            jnp.concatenate([blocks[k + e * 4][n * 64:(n + 1) * 64] for n in range(4)], axis=1)
            for k in range(4) for e in range(2)
        ], axis=0)
        for which in range(2):
            span = slice(256 + which * 40, 256 + (which + 1) * 40)
            text = jnp.concatenate([b[span].astype(f32) for b in blocks], axis=0)
            keep_ref[which] = jnp.where(core == 0, text[:, :HW], text[:, HW:]).astype(bf16)
        text_ref = keep_ref
        qkv = jnp.dot(rows, w_ref[...], preferred_element_type=f32)
    else:
        mine = jnp.concatenate([b[...] for b in blocks[:4]], axis=0)
        other = jnp.concatenate([b[...] for b in blocks[4:]], axis=0)
        w_mine = w_ref[pl.ds(pl.multiple_of(core * HALF, HALF), HALF), :]
        w_other = w_ref[pl.ds(pl.multiple_of((1 - core) * HALF, HALF), HALF), :]
        qkv = jnp.dot(mine, w_mine, preferred_element_type=f32)
        qkv = qkv + jnp.dot(other, w_other, preferred_element_type=f32)
    scale = HEAD_DIM ** (-0.5)
    q01[...] = (qkv[:, 0:128] * scale).astype(bf16)
    k01[0:TOK, :] = qkv[:, 128:256].astype(bf16)
    v01[0:TOK, :] = qkv[:, 256:384].astype(bf16)
    q2[...] = (qkv[:, 384:448] * scale).astype(bf16)
    k2[0:TOK, :] = qkv[:, 448:512].astype(bf16)
    v2[0:TOK, :] = qkv[:, 512:576].astype(bf16)
    k01[TOK:, :] = text_ref[0, :, 0:128]
    v01[TOK:, :] = text_ref[1, :, 0:128]
    k2[TOK:, :] = text_ref[0, :, 128:192]
    v2[TOK:, :] = text_ref[1, :, 128:192]
    lane = lax.broadcasted_iota(jnp.int32, (128, 128), 1)

    def attend(query, keys, values):
        scores = lax.dot_general(
            query, keys, (((1,), (1,)), ((), ())), preferred_element_type=f32
        )
        top = jnp.max(scores, axis=-1, keepdims=True)
        exp_scores = jnp.exp(scores - top)
        total = jnp.sum(exp_scores, axis=-1, keepdims=True)
        weights = (exp_scores * (1.0 / total)).astype(bf16)
        return jnp.dot(weights, values, preferred_element_type=f32)

    for chunk in range(4):
        span = slice(chunk * 128, (chunk + 1) * 128)
        pair = q01[span, :]
        zero = jnp.zeros_like(pair)
        out0 = attend(jnp.where(lane < 64, pair, zero), k01[...], v01[...])
        out1 = attend(jnp.where(lane < 64, zero, pair), k01[...], v01[...])
        out01 = jnp.where(lane < 64, out0, out1).astype(bf16)
        out2 = attend(q2[span, :], k2[...], v2[...])
        from_x = lax.rem(x - chunk + 4, 4)
        for part in range(8):
            if first:
                sub = part % 4
                zh = core if part < 4 else 1 - core
            else:
                sub, zh = part // 2, part % 2
            target = (sub * 4 + from_x) * 2 + zh
            out_ref[target, 0:16] = out01[part * 16:(part + 1) * 16]
            out_ref[target, 16:24] = jnp.concatenate(
                [out2[part * 16:part * 16 + 8], out2[part * 16 + 8:(part + 1) * 16]], axis=1
            ).astype(bf16)


def terms_kernel(first, place_ref, att_ref, *refs):
    if first:
        messages, (part_ref, total_ref, mod_ref) = refs[:4], refs[4:]
        for k in range(4):
            from_zl = lax.rem(place_ref[1] - k + 4, 4)
            for core in range(2):
                mod_ref[from_zl * 2 + core] = messages[k][core]
        lat_ref = mod_ref
    else:
        lat_ref, mod_ref, part_ref, total_ref = refs
    run = jnp.where(place_ref[0] == 0, lat_ref[0, 0:16], 0.0)
    for j in range(8):
        part_ref[j] = run
        sub, zh = j // 2, j % 2
        pieces = []
        for k in range(4):
            piece = att_ref[(sub * 4 + k) * 2 + zh].astype(f32)
            tail = jnp.concatenate([piece[16:24, 0:64], piece[16:24, 64:128]], axis=0)
            pieces += [piece[0:16], tail]
        attended = jnp.concatenate(pieces, axis=1)
        run = run + mod_ref[j, 19:20] * (lat_ref[j, 0:16] + mod_ref[j, 18:19] * attended)
    for k in range(4):
        total_ref[k] = run


def later_offset(place_ref, totals_ref):
    offset = jnp.zeros((16, HALF), f32)
    for k in range(3):
        offset = offset + jnp.where(k < place_ref[0], totals_ref[k], 0.0)
    return offset


def change_kernel(place_ref, part_ref, lat_ref, totals_ref, chg_ref):
    offset = later_offset(place_ref, totals_ref)
    for j in range(8):
        change = jnp.max(jnp.abs(part_ref[j] + offset - lat_ref[j, 0:16]))
        chg_ref[j:j + 1, :] = jnp.full((1, 128), change, f32)


def new_kernel(place_ref, part_ref, totals_ref, after_ref, new_ref):
    offset = later_offset(place_ref, totals_ref)
    for j in range(8):
        new_ref[j] = part_ref[j] + offset


def update_kernel(place_ref, part_ref, lat_ref, totals_ref, new_ref, chg_ref, stats_ref):
    offset = later_offset(place_ref, totals_ref)
    lane = lax.broadcasted_iota(jnp.int32, (16, 128), 1)
    for j in range(8):
        new = part_ref[j] + offset
        new_ref[j] = new
        change = jnp.max(jnp.abs(new - lat_ref[j, 0:16]))
        chg_ref[j:j + 1, :] = jnp.full((1, 128), change, f32)
        average = jnp.mean(new, axis=-1, keepdims=True)
        centred = new - average
        spread = jnp.sum(centred * centred, axis=-1, keepdims=True)
        stats_ref[j] = jnp.where(lane == 0, average, spread)


def modulate_kernel(new_ref, mine_ref, other_ref, mod_ref, out_ref):
    for j in range(8):
        mean_a, mean_b = mine_ref[j][:, 0:1], other_ref[j][:, 0:1]
        spread = mine_ref[j][:, 1:2] + other_ref[j][:, 1:2]
        average = (mean_a + mean_b) * 0.5
        gap = mean_a - mean_b
        variance = (spread + gap * gap * (HALF * 0.5)) * (1.0 / D)
        normed = (new_ref[j] - average) * lax.rsqrt(variance + 1e-06)
        out_ref[j] = (
            normed * (1.0 + mod_ref[j, 17:18]) + mod_ref[j, 16:17]
        ).astype(bf16)


def place_kernel(in_ref, out_ref):
    for sub in range(4):
        for k in range(4):
            cols = slice(k * HW, (k + 1) * HW)
            out_ref[sub * 16:(sub + 1) * 16, k * 2 * HW:(k + 1) * 2 * HW] = jnp.concatenate(
                [in_ref[sub * 2][:, cols], in_ref[sub * 2 + 1][:, cols]], axis=1
            )


def on_device(states, qkv_weight, text_kv, mod_table, step_table, step_ids):
    y, zl, c, x, zh = (lax.axis_index(name) for name in AXES)
    same = c == zh
    place = jnp.stack([y, zl, c, x]).astype(jnp.int32)

    with jax.named_scope("start"):
        mod_own = lax.dynamic_index_in_dim(mod_table, step_ids[0], 0, keepdims=False)
        packed, keep, mate = call(
            start_kernel,
            (struct(4, 144, BLOCK, dtype=bf16), struct(4, 24, HALF), struct(4, 24, HALF)),
            3, 3,
        )(place, step_ids, step_table, states, mod_own, text_kv)
    with jax.named_scope("weights"):
        w = call(columns_kernel, struct(48, 3 * HW, dtype=bf16), 1, 0, after=1)(
            qkv_weight, packed
        )
        w_b = [permute(w, ("c", "zh"), lambda p, k=k: {"c": p["zh"], "zh": 1 - p["zh"]}
                       if p["c"] == k else None) for k in range(2)]
        w_a = permute(w, ("c", "zh"), lambda p: None if p["c"] == p["zh"] else
                      {"c": 1 - p["c"], "zh": p["zh"]})
        w0 = jnp.where(same, jnp.where(c == 0, w, w_a), w_b[0])
        w1 = jnp.where(same, jnp.where(c == 1, w, w_a), w_b[1])
        w2 = jnp.concatenate([w0, w1], axis=0)
        w8 = jnp.stack([w2, shift_z(w2, 1), shift_z(w2, 2), shift_z(w2, -1)])

    with jax.named_scope("gather_first"):
        packed = swap_core_zh(packed, same)
        sends = call(send_kernel, (struct(336, BLOCK, dtype=bf16),) * 4, 1, 1)(place, packed)
        mine = [sends[0]] + [shift(sends[k], "x", k) for k in (1, 2, 3)]
        blocks = mine + [shift(b, "c", 1) for b in mine]

    with jax.named_scope("weights_y"):
        w_next, w_last = shift(w8, "y", 1), shift(w8, "y", -1)
        far_a, far_b = shift(w_next[:2], "y", 1), shift(w_last[2:], "y", -1)
        pieces = (w8, w_next, far_a, far_b, w_last)

    with jax.named_scope("states"):
        messages = call(message_kernel, (struct(2, 24, HALF),) * 4, 2, 1, after=1)(
            place, keep, shift(mate, "c", 1), far_b
        )
        messages = [messages[0]] + [shift(messages[k], "zl", k) for k in (1, 2, 3)]

    with jax.named_scope("weights_y"):
        weight = call(weight_kernel, struct(D, 3 * HW, dtype=bf16), 5, 1)(place, *pieces)

    text = None
    for sweep in range(SWEEPS):
        last = sweep == SWEEPS - 1
        with jax.named_scope("attention"):
            outs = (struct(32, 24, 128, dtype=bf16),)
            scratch = [
                pltpu.VMEM((KEYS, 128), bf16), pltpu.VMEM((KEYS, 128), bf16),
                pltpu.VMEM((KEYS, 64), bf16), pltpu.VMEM((KEYS, 64), bf16),
                pltpu.VMEM((TOK, 128), bf16), pltpu.VMEM((TOK, 64), bf16),
            ]
            if sweep == 0:
                operands = (*blocks, weight)
                outs = outs + (struct(2, TXT, HW, dtype=bf16),)
            else:
                operands = (*blocks, weight, text)
            spaces = [pltpu.SMEM] + [pltpu.VMEM] * len(operands)
            attended, *text_out = pl.pallas_call(
                functools.partial(attention_kernel, sweep == 0),
                out_shape=outs,
                in_specs=[pl.BlockSpec(memory_space=space) for space in spaces],
                out_specs=tuple(pl.BlockSpec(memory_space=pltpu.VMEM) for _ in outs),
                compiler_params=pltpu.CompilerParams(vmem_limit_bytes=20 * MIB),
                cost_estimate=pl.CostEstimate(
                    flops=2 * TOK * D * 3 * HW + 4 * TOK * KEYS * HW,
                    bytes_accessed=24 << 20, transcendentals=3 * TOK * KEYS,
                ),
                scratch_shapes=scratch,
            )(place, *operands)
            text = text_out[0] if text_out else text
        with jax.named_scope("to_prefix"):
            if sweep == 0:
                attended = call(hold_kernel, struct(32, 24, 128, dtype=bf16), 1, 0, after=3)(
                    attended, *messages[1:]
                )
            attended = lax.all_to_all(attended, ("zl", "x", "zh"), 0, 0)
        with jax.named_scope("prefix"):
            outs = (struct(8, 16, HALF), struct(4, 16, HALF))
            if sweep == 0:
                part, total, mods = call(
                    functools.partial(terms_kernel, True), outs + (struct(8, 24, HALF),), 5, 1
                )(place, attended, *messages)
                lat = mods
            else:
                part, total = call(functools.partial(terms_kernel, False), outs, 3, 1)(
                    place, attended, lat, mods
                )
            totals = lax.all_to_all(total, "y", 0, 0)
            if last:
                break
            lat, change, stats = call(
                update_kernel, (struct(8, 16, HALF), struct(8, 128), struct(8, 16, 128)), 3, 1
            )(place, part, lat, totals)
        if not last:
            with jax.named_scope("norm"):
                modulated = call(
                    modulate_kernel, struct(8, 16, HALF, dtype=bf16), 4, 0
                )(lat, stats, shift(stats, "c", 1), mods)
            with jax.named_scope("gather"):
                modulated = lax.all_to_all(modulated, ("zl", "zh"), 0, 0).reshape(128, HALF)
                mine = [modulated] + [shift(modulated, "x", k) for k in (1, 2, 3)]
                blocks = mine + [shift(b, "c", 1) for b in mine]
    with jax.named_scope("changes"):
        top = call(change_kernel, struct(8, 128), 3, 1)(place, part, lat, totals)
        top = jnp.concatenate([change, top], axis=0)
        top = functools.reduce(jnp.maximum, [top] + [shift(top, "zl", k) for k in (1, 2, 3)])
    with jax.named_scope("place"):
        out = call(new_kernel, struct(8, 16, HALF), 2, 1, after=1)(place, part, totals, top)
        out = lax.all_to_all(out, ("zl", "c"), 0, 0)
        out = call(place_kernel, struct(ROWS, D), 1, 0)(out)
    with jax.named_scope("changes"):
        top = jnp.maximum(top, shift(top, "zh", 1))
        top = functools.reduce(jnp.maximum, [top] + [shift(top, "x", k) for k in (1, 2, 3)])
        top = jnp.maximum(top, shift(top, "c", 1))
        top = top[:, 0].reshape(SWEEPS, 8)
        top = lax.dynamic_slice_in_dim(top, zl * 2 + c, 1, axis=1)
    return out[None], top


def solution(mesh):
    fine = Mesh(mesh.devices.reshape([SIZES[name] for name in AXES]), AXES)
    tm, seq = ("y", "zl", "c"), ("x", "zh")
    in_specs = (
        P(tm, seq, None), P(tm, None, seq), P(tm, seq, None, None), P(), P(), P(tm),
    )
    out_specs = (P(tm, seq, None), P(None, tm))
    return jax.shard_map(
        on_device, mesh=fine, in_specs=in_specs, out_specs=out_specs, check_vma=False
    )
```

```python
import functools
import itertools

import jax
import jax.numpy as jnp
from jax import lax
from jax.experimental import pallas as pl
from jax.experimental.pallas import tpu as pltpu
from jax.sharding import Mesh, PartitionSpec as P

AXES = ("y", "zl", "c", "x", "zh")
SIZES = {"y": 4, "zl": 4, "c": 2, "x": 4, "zh": 2}

HEAD_DIM = 64
SWEEPS = 2
D = 1536
HALF = 768
BLOCK = 384
HW = 192
ROWS = 64
TOK = 512
TXT = 320
KEYS = TOK + TXT
MIB = 1024 * 1024
f32, bf16 = jnp.float32, jnp.bfloat16


def permute(value, axes, move):
    def index(place):
        flat = 0
        for name in axes:
            flat = flat * SIZES[name] + place[name] % SIZES[name]
        return flat

    pairs = []
    for coords in itertools.product(*[range(SIZES[name]) for name in axes]):
        place = dict(zip(axes, coords))
        target = move(dict(place))
        if target is not None:
            pairs.append((index(place), index(target)))
    return lax.ppermute(value, axes if len(axes) > 1 else axes[0], pairs)


def shift(value, axis, amount):
    return permute(value, (axis,), lambda p: {axis: p[axis] + amount})


def shift_z(value, amount):
    def move(p):
        ring = (p["zh"] * 4 + p["zl"] + amount) % 8
        return {"zl": ring % 4, "zh": ring // 4}

    return permute(value, ("zl", "zh"), move)


def swap_core_zh(value, same):
    moved = permute(
        value, ("c", "zh"),
        lambda p: None if p["c"] == p["zh"] else {"c": p["zh"], "zh": p["c"]},
    )
    return jnp.where(same, value, moved)


def call(kernel, out_shape, n_vmem, n_smem, limit=6, after=0):
    return pl.pallas_call(
        kernel,
        out_shape=out_shape,
        in_specs=[pl.BlockSpec(memory_space=pltpu.SMEM)] * n_smem
        + [pl.BlockSpec(memory_space=pltpu.VMEM)] * n_vmem
        + [pl.BlockSpec(memory_space=pl.ANY)] * after,
        out_specs=jax.tree.map(lambda _: pl.BlockSpec(memory_space=pltpu.VMEM), out_shape),
        compiler_params=pltpu.CompilerParams(vmem_limit_bytes=limit * MIB),
    )


def struct(*shape, dtype=f32):
    return jax.ShapeDtypeStruct(shape, dtype)


def half_columns(half):
    return [slice(k * 2 * HW + half * HW, k * 2 * HW + (half + 1) * HW) for k in range(4)]


def columns_kernel(w_ref, out_ref):
    raw = w_ref[...].astype(f32)
    parts = [raw[:, k, :128] for k in range(3)] + [raw[:, k, 128:] for k in range(3)]
    out_ref[...] = jnp.concatenate(parts, axis=1).astype(bf16)


def start_kernel(place_ref, ids_ref, steps_ref, lat_ref, mod_ref, text_ref, after_ref,
                 out_ref, keep_ref, mate_ref):
    latent = lat_ref[0]
    average = jnp.mean(latent, axis=-1, keepdims=True)
    centred = latent - average
    variance = jnp.mean(centred * centred, axis=-1, keepdims=True)
    normed = centred * lax.rsqrt(variance + 1e-06)
    modulated = (normed * (1.0 + mod_ref[1:2, :]) + mod_ref[0:1, :]).astype(bf16)
    raw = text_ref[0].astype(f32)
    rows = jnp.concatenate([raw[:, 0, :], raw[:, 1, :]], axis=0).astype(bf16)
    step = jnp.full((5, HALF), -steps_ref[ids_ref[0]], f32)
    for half in range(2):
        piece = jnp.concatenate([modulated[:, s] for s in half_columns(half)], axis=1)
        out_ref[half * 2, 0:64] = piece[:, 0:BLOCK]
        out_ref[half * 2 + 1, 0:64] = piece[:, BLOCK:]
        piece = jnp.concatenate([latent[:, s] for s in half_columns(half)], axis=1)
        mods = jnp.concatenate([mod_ref[:, s] for s in half_columns(half)], axis=1)
        below = jnp.concatenate([mods, step], axis=0)
        for ref, wanted in ((keep_ref, place_ref[2]), (mate_ref, 1 - place_ref[2])):
            @pl.when(wanted == half)
            def _(ref=ref, piece=piece, below=below):
                for sub in range(4):
                    ref[sub, 0:16] = piece[sub * 16:(sub + 1) * 16]
                    ref[sub, 16:24] = below
    for k in range(4):
        out_ref[k, 64:144] = rows[:, k * BLOCK:(k + 1) * BLOCK]


def hold_kernel(in_ref, *refs):
    refs[-1][...] = in_ref[...]


def message_kernel(place_ref, keep_ref, mate_ref, extra_ref, *out_refs):
    zl, core = place_ref[1], place_ref[2]
    if len(out_refs) == 5:
        out_refs[4][...] = extra_ref[...]
    for k in range(4):
        target = lax.rem(zl + k, 4)
        out_refs[k][core] = keep_ref[target]
        out_refs[k][1 - core] = mate_ref[target]


def send_kernel(place_ref, in_ref, *out_refs):
    x = place_ref[3]
    for k in range(4):
        for block in range(4):
            out_refs[k][block * 64:(block + 1) * 64] = in_ref[block, 0:64]
        out_refs[k][256:336] = in_ref[lax.rem(x + k, 4), 64:144]


def weight_kernel(place_ref, *refs):
    y, zl = place_ref[0], place_ref[1]
    for piece, ky in enumerate((0, 1, -1, 2)):
        from_y = lax.rem(y - ky + 4, 4)
        for kz in range(4):
            from_zl = lax.rem(zl - kz + 4, 4)
            row = (from_zl // 2) * HALF + from_y * HW + lax.rem(from_zl, 2) * 96
            refs[4][pl.ds(pl.multiple_of(row, 32), 96), :] = refs[piece][kz]


def attention_kernel(first, place_ref, *refs):
    blocks, refs = refs[:8], refs[8:]
    if first:
        w_ref, out_ref, keep_ref, k01, v01, k2, v2, q01, q2 = refs
    else:
        w_ref, text_ref, out_ref, k01, v01, k2, v2, q01, q2 = refs
    core, x = place_ref[2], place_ref[3]
    if first:
        rows = jnp.concatenate([
            jnp.concatenate([blocks[k + e * 4][n * 64:(n + 1) * 64] for n in range(4)], axis=1)
            for k in range(4) for e in range(2)
        ], axis=0)
        for which in range(2):
            span = slice(256 + which * 40, 256 + (which + 1) * 40)
            text = jnp.concatenate([b[span].astype(f32) for b in blocks], axis=0)
            keep_ref[which] = jnp.where(core == 0, text[:, :HW], text[:, HW:]).astype(bf16)
        text_ref = keep_ref
        qkv = jnp.dot(rows, w_ref[...], preferred_element_type=f32)
    else:
        mine = jnp.concatenate([b[...] for b in blocks[:4]], axis=0)
        other = jnp.concatenate([b[...] for b in blocks[4:]], axis=0)
        w_mine = w_ref[pl.ds(pl.multiple_of(core * HALF, HALF), HALF), :]
        w_other = w_ref[pl.ds(pl.multiple_of((1 - core) * HALF, HALF), HALF), :]
        qkv = jnp.dot(mine, w_mine, preferred_element_type=f32)
        qkv = qkv + jnp.dot(other, w_other, preferred_element_type=f32)
    scale = HEAD_DIM ** (-0.5)
    q01[...] = (qkv[:, 0:128] * scale).astype(bf16)
    k01[0:TOK, :] = qkv[:, 128:256].astype(bf16)
    v01[0:TOK, :] = qkv[:, 256:384].astype(bf16)
    q2[...] = (qkv[:, 384:448] * scale).astype(bf16)
    k2[0:TOK, :] = qkv[:, 448:512].astype(bf16)
    v2[0:TOK, :] = qkv[:, 512:576].astype(bf16)
    k01[TOK:, :] = text_ref[0, :, 0:128]
    v01[TOK:, :] = text_ref[1, :, 0:128]
    k2[TOK:, :] = text_ref[0, :, 128:192]
    v2[TOK:, :] = text_ref[1, :, 128:192]
    lane = lax.broadcasted_iota(jnp.int32, (TOK, 128), 1)

    def attend(query, keys, values):
        scores = lax.dot_general(
            query, keys, (((1,), (1,)), ((), ())), preferred_element_type=f32
        )
        top = jnp.max(scores, axis=-1, keepdims=True)
        exp_scores = jnp.exp(scores - top)
        total = jnp.sum(exp_scores, axis=-1, keepdims=True)
        weights = (exp_scores * (1.0 / total)).astype(bf16)
        return jnp.dot(weights, values, preferred_element_type=f32)

    pair = q01[...]
    zero = jnp.zeros_like(pair)
    out0 = attend(jnp.where(lane < 64, pair, zero), k01[...], v01[...])
    out1 = attend(jnp.where(lane < 64, zero, pair), k01[...], v01[...])
    out01 = jnp.where(lane < 64, out0, out1).astype(bf16)
    out2 = attend(q2[...], k2[...], v2[...])
    for part in range(TOK // 16):
        slot, place = part // 8, part % 8
        if first:
            sub, zh = place % 4, (core if place < 4 else 1 - core)
        else:
            sub, zh = place // 2, place % 2
        target = (sub * 4 + lax.rem(x - slot + 4, 4)) * 2 + zh
        start = part * 16
        out_ref[target, 0:16] = out01[start:start + 16]
        out_ref[target, 16:24] = jnp.concatenate(
            [out2[start:start + 8], out2[start + 8:start + 16]], axis=1
        ).astype(bf16)


def terms_kernel(first, place_ref, att_ref, *refs):
    if first:
        messages, (part_ref, total_ref, mod_ref) = refs[:4], refs[4:]
        for k in range(4):
            from_zl = lax.rem(place_ref[1] - k + 4, 4)
            for core in range(2):
                mod_ref[from_zl * 2 + core] = messages[k][core]
        lat_ref = mod_ref
    else:
        lat_ref, mod_ref, part_ref, total_ref = refs
    run = jnp.where(place_ref[0] == 0, lat_ref[0, 0:16], 0.0)
    for j in range(8):
        part_ref[j] = run
        sub, zh = j // 2, j % 2
        pieces = []
        for k in range(4):
            piece = att_ref[(sub * 4 + k) * 2 + zh].astype(f32)
            tail = jnp.concatenate([piece[16:24, 0:64], piece[16:24, 64:128]], axis=0)
            pieces += [piece[0:16], tail]
        attended = jnp.concatenate(pieces, axis=1)
        run = run + mod_ref[j, 19:20] * (lat_ref[j, 0:16] + mod_ref[j, 18:19] * attended)
    for k in range(4):
        total_ref[k] = run


def later_offset(place_ref, totals_ref):
    offset = jnp.zeros((16, HALF), f32)
    for k in range(3):
        offset = offset + jnp.where(k < place_ref[0], totals_ref[k], 0.0)
    return offset


def final_kernel(place_ref, part_ref, lat_ref, totals_ref, chg_ref, keep_ref, mate_ref):
    offset = later_offset(place_ref, totals_ref)
    core = place_ref[2]
    for j in range(8):
        new = part_ref[j] + offset
        chg_ref[j:j + 1, :] = jnp.full((1, 128), jnp.max(jnp.abs(new - lat_ref[j])), f32)
        for ref, wanted in ((keep_ref, core), (mate_ref, 1 - core)):
            @pl.when(wanted == j % 2)
            def _(ref=ref, new=new, j=j):
                ref[j // 2] = new


def update_kernel(place_ref, part_ref, lat_ref, totals_ref, new_ref, chg_ref, stats_ref):
    offset = later_offset(place_ref, totals_ref)
    lane = lax.broadcasted_iota(jnp.int32, (16, 128), 1)
    for j in range(8):
        new = part_ref[j] + offset
        new_ref[j] = new
        change = jnp.max(jnp.abs(new - lat_ref[j, 0:16]))
        chg_ref[j:j + 1, :] = jnp.full((1, 128), change, f32)
        average = jnp.mean(new, axis=-1, keepdims=True)
        centred = new - average
        spread = jnp.sum(centred * centred, axis=-1, keepdims=True)
        stats_ref[j] = jnp.where(lane == 0, average, spread)


def modulate_kernel(new_ref, mine_ref, other_ref, mod_ref, out_ref):
    for j in range(8):
        mean_a, mean_b = mine_ref[j][:, 0:1], other_ref[j][:, 0:1]
        spread = mine_ref[j][:, 1:2] + other_ref[j][:, 1:2]
        average = (mean_a + mean_b) * 0.5
        gap = mean_a - mean_b
        variance = (spread + gap * gap * (HALF * 0.5)) * (1.0 / D)
        normed = (new_ref[j] - average) * lax.rsqrt(variance + 1e-06)
        out_ref[j] = (
            normed * (1.0 + mod_ref[j, 17:18]) + mod_ref[j, 16:17]
        ).astype(bf16)


def place_kernel(place_ref, *refs):
    out_ref = refs[4]
    for k in range(4):
        row = pl.multiple_of(lax.rem(place_ref[1] - k + 4, 4) * 16, 16)
        for x in range(4):
            cols = slice(x * HW, (x + 1) * HW)
            out_ref[pl.ds(row, 16), x * 2 * HW:(x + 1) * 2 * HW] = jnp.concatenate(
                [refs[k][0][:, cols], refs[k][1][:, cols]], axis=1
            )


def on_device(states, qkv_weight, text_kv, mod_table, step_table, step_ids):
    y, zl, c, x, zh = (lax.axis_index(name) for name in AXES)
    same = c == zh
    place = jnp.stack([y, zl, c, x]).astype(jnp.int32)

    with jax.named_scope("weights"):
        w = call(columns_kernel, struct(48, 3 * HW, dtype=bf16), 1, 0)(qkv_weight)
        w_b = [permute(w, ("c", "zh"), lambda p, k=k: {"c": p["zh"], "zh": 1 - p["zh"]}
                       if p["c"] == k else None) for k in range(2)]
        w_a = permute(w, ("c", "zh"), lambda p: None if p["c"] == p["zh"] else
                      {"c": 1 - p["c"], "zh": p["zh"]})
        w0 = jnp.where(same, jnp.where(c == 0, w, w_a), w_b[0])
        w1 = jnp.where(same, jnp.where(c == 1, w, w_a), w_b[1])
        w2 = jnp.concatenate([w0, w1], axis=0)
        w8 = jnp.stack([w2, shift_z(w2, 1), shift_z(w2, 2), shift_z(w2, -1)])

    with jax.named_scope("start"):
        mod_own = lax.dynamic_index_in_dim(mod_table, step_ids[0], 0, keepdims=False)
        packed, keep, mate = call(
            start_kernel,
            (struct(4, 144, BLOCK, dtype=bf16), struct(4, 24, HALF), struct(4, 24, HALF)),
            3, 3, after=1,
        )(place, step_ids, step_table, states, mod_own, text_kv, w8)
    with jax.named_scope("gather_first"):
        packed = swap_core_zh(packed, same)
        sends = call(send_kernel, (struct(336, BLOCK, dtype=bf16),) * 4, 1, 1)(place, packed)
        mine = [sends[0]] + [shift(sends[k], "x", k) for k in (1, 2, 3)]
        blocks = mine + [shift(b, "c", 1) for b in mine]

    with jax.named_scope("weights_y"):
        pieces = [w8] + [shift(w8, "y", k) for k in (1, -1, 2)]

    with jax.named_scope("states"):
        messages = call(message_kernel, (struct(2, 24, HALF),) * 4, 2, 1, after=1)(
            place, keep, shift(mate, "c", 1), pieces[2]
        )
        messages = [messages[0]] + [shift(messages[k], "zl", k) for k in (1, 2, 3)]

    with jax.named_scope("weights_y"):
        weight = call(weight_kernel, struct(D, 3 * HW, dtype=bf16), 4, 1)(place, *pieces)

    text = None
    for sweep in range(SWEEPS):
        last = sweep == SWEEPS - 1
        with jax.named_scope("attention"):
            outs = (struct(32, 24, 128, dtype=bf16),)
            scratch = [
                pltpu.VMEM((KEYS, 128), bf16), pltpu.VMEM((KEYS, 128), bf16),
                pltpu.VMEM((KEYS, 64), bf16), pltpu.VMEM((KEYS, 64), bf16),
                pltpu.VMEM((TOK, 128), bf16), pltpu.VMEM((TOK, 64), bf16),
            ]
            if sweep == 0:
                operands = (*blocks, weight)
                outs = outs + (struct(2, TXT, HW, dtype=bf16),)
            else:
                operands = (*blocks, weight, text)
            spaces = [pltpu.SMEM] + [pltpu.VMEM] * len(operands)
            attended, *text_out = pl.pallas_call(
                functools.partial(attention_kernel, sweep == 0),
                out_shape=outs,
                in_specs=[pl.BlockSpec(memory_space=space) for space in spaces],
                out_specs=tuple(pl.BlockSpec(memory_space=pltpu.VMEM) for _ in outs),
                compiler_params=pltpu.CompilerParams(vmem_limit_bytes=24 * MIB),
                cost_estimate=pl.CostEstimate(
                    flops=2 * TOK * D * 3 * HW + 4 * TOK * KEYS * HW,
                    bytes_accessed=24 << 20, transcendentals=3 * TOK * KEYS,
                ),
                scratch_shapes=scratch,
            )(place, *operands)
            text = text_out[0] if text_out else text
        with jax.named_scope("to_prefix"):
            if sweep == 0:
                attended = call(hold_kernel, struct(32, 24, 128, dtype=bf16), 1, 0, after=3)(
                    attended, *messages[1:]
                )
            attended = lax.all_to_all(attended, ("zl", "x", "zh"), 0, 0)
        with jax.named_scope("prefix"):
            outs = (struct(8, 16, HALF), struct(4, 16, HALF))
            if sweep == 0:
                part, total, mods = call(
                    functools.partial(terms_kernel, True), outs + (struct(8, 24, HALF),), 5, 1
                )(place, attended, *messages)
                lat = mods
            else:
                part, total = call(functools.partial(terms_kernel, False), outs, 3, 1)(
                    place, attended, lat, mods
                )
            totals = lax.all_to_all(total, "y", 0, 0)
            if last:
                break
            lat, change, stats = call(
                update_kernel, (struct(8, 16, HALF), struct(8, 128), struct(8, 16, 128)), 3, 1
            )(place, part, lat, totals)
        if not last:
            with jax.named_scope("norm"):
                modulated = call(
                    modulate_kernel, struct(8, 16, HALF, dtype=bf16), 4, 0
                )(lat, stats, shift(stats, "c", 1), mods)
            with jax.named_scope("gather"):
                modulated = lax.all_to_all(modulated, ("zl", "zh"), 0, 0).reshape(128, HALF)
                mine = [modulated] + [shift(modulated, "x", k) for k in (1, 2, 3)]
                blocks = mine + [shift(b, "c", 1) for b in mine]
    with jax.named_scope("place"):
        top, keep, mate = call(
            final_kernel, (struct(8, 128), struct(4, 16, HALF), struct(4, 16, HALF)), 3, 1
        )(place, part, lat, totals)
        top = jnp.concatenate([change, top], axis=0)
        top = jnp.maximum(top, shift(top, "c", 1))
        *outs, top = call(
            message_kernel, (struct(2, 16, HALF),) * 4 + (struct(16, 128),), 3, 1
        )(place, keep, shift(mate, "c", 1), top)
        outs = [outs[0]] + [shift(outs[k], "zl", k) for k in (1, 2, 3)]
        out = call(place_kernel, struct(ROWS, D), 4, 1)(place, *outs)
    with jax.named_scope("changes"):
        top = functools.reduce(jnp.maximum, [top] + [shift(top, "zl", k) for k in (1, 2, 3)])
        top = functools.reduce(jnp.maximum, [top] + [shift(top, "x", k) for k in (1, 2, 3)])
        top = jnp.maximum(top, shift(top, "zh", 1))
        top = top[:, 0].reshape(SWEEPS, 8)
        top = lax.dynamic_slice_in_dim(top, zl * 2 + c, 1, axis=1)
    return out[None], top


def solution(mesh):
    fine = Mesh(mesh.devices.reshape([SIZES[name] for name in AXES]), AXES)
    tm, seq = ("y", "zl", "c"), ("x", "zh")
    in_specs = (
        P(tm, seq, None), P(tm, None, seq), P(tm, seq, None, None), P(), P(), P(tm),
    )
    out_specs = (P(tm, seq, None), P(None, tm))
    return jax.shard_map(
        on_device, mesh=fine, in_specs=in_specs, out_specs=out_specs, check_vma=False
    )
```

```python
import functools
import itertools

import jax
import jax.numpy as jnp
from jax import lax
from jax.experimental import pallas as pl
from jax.experimental.pallas import tpu as pltpu
from jax.sharding import Mesh, PartitionSpec as P

AXES = ("y", "zl", "c", "x", "zh")
SIZES = {"y": 4, "zl": 4, "c": 2, "x": 4, "zh": 2}

HEAD_DIM = 64
SWEEPS = 2
D = 1536
HALF = 768
BLOCK = 384
HW = 192
ROWS = 64
TOK = 512
TXT = 320
KEYS = TOK + TXT
MIB = 1024 * 1024
f32, bf16 = jnp.float32, jnp.bfloat16


def permute(value, axes, move):
    def index(place):
        flat = 0
        for name in axes:
            flat = flat * SIZES[name] + place[name] % SIZES[name]
        return flat

    pairs = []
    for coords in itertools.product(*[range(SIZES[name]) for name in axes]):
        place = dict(zip(axes, coords))
        target = move(dict(place))
        if target is not None:
            pairs.append((index(place), index(target)))
    return lax.ppermute(value, axes if len(axes) > 1 else axes[0], pairs)


def shift(value, axis, amount):
    return permute(value, (axis,), lambda p: {axis: p[axis] + amount})


def shift_z(value, amount):
    def move(p):
        ring = (p["zh"] * 4 + p["zl"] + amount) % 8
        return {"zl": ring % 4, "zh": ring // 4}

    return permute(value, ("zl", "zh"), move)


def swap_core_zh(value, same):
    moved = permute(
        value, ("c", "zh"),
        lambda p: None if p["c"] == p["zh"] else {"c": p["zh"], "zh": p["c"]},
    )
    return jnp.where(same, value, moved)


def call(kernel, out_shape, n_vmem, n_smem, limit=6, after=0):
    return pl.pallas_call(
        kernel,
        out_shape=out_shape,
        in_specs=[pl.BlockSpec(memory_space=pltpu.SMEM)] * n_smem
        + [pl.BlockSpec(memory_space=pltpu.VMEM)] * n_vmem
        + [pl.BlockSpec(memory_space=pl.ANY)] * after,
        out_specs=jax.tree.map(lambda _: pl.BlockSpec(memory_space=pltpu.VMEM), out_shape),
        compiler_params=pltpu.CompilerParams(vmem_limit_bytes=limit * MIB),
    )


def struct(*shape, dtype=f32):
    return jax.ShapeDtypeStruct(shape, dtype)


def half_columns(half):
    return [slice(k * 2 * HW + half * HW, k * 2 * HW + (half + 1) * HW) for k in range(4)]


def columns_kernel(w_ref, out_ref):
    parts = [w_ref[k, :, :128] for k in range(3)] + [w_ref[k, :, 128:] for k in range(3)]
    out_ref[...] = jnp.concatenate(parts, axis=1)


def start_kernel(place_ref, ids_ref, steps_ref, lat_ref, mod_ref, text_ref,
                 out_ref, keep_ref, mate_ref):
    latent = lat_ref[0]
    average = jnp.mean(latent, axis=-1, keepdims=True)
    centred = latent - average
    variance = jnp.mean(centred * centred, axis=-1, keepdims=True)
    normed = centred * lax.rsqrt(variance + 1e-06)
    modulated = (normed * (1.0 + mod_ref[1:2, :]) + mod_ref[0:1, :]).astype(bf16)
    raw = text_ref[0].astype(f32)
    rows = jnp.concatenate([raw[:, 0, :], raw[:, 1, :]], axis=0).astype(bf16)
    step = jnp.full((5, HALF), -steps_ref[ids_ref[0]], f32)
    for half in range(2):
        piece = jnp.concatenate([modulated[:, s] for s in half_columns(half)], axis=1)
        out_ref[half * 2, 0:64] = piece[:, 0:BLOCK]
        out_ref[half * 2 + 1, 0:64] = piece[:, BLOCK:]
        piece = jnp.concatenate([latent[:, s] for s in half_columns(half)], axis=1)
        mods = jnp.concatenate([mod_ref[:, s] for s in half_columns(half)], axis=1)
        below = jnp.concatenate([mods, step], axis=0)
        for ref, wanted in ((keep_ref, place_ref[2]), (mate_ref, 1 - place_ref[2])):
            @pl.when(wanted == half)
            def _(ref=ref, piece=piece, below=below):
                for sub in range(4):
                    ref[sub, 0:16] = piece[sub * 16:(sub + 1) * 16]
                    ref[sub, 16:24] = below
    for k in range(4):
        out_ref[k, 64:144] = rows[:, k * BLOCK:(k + 1) * BLOCK]


def hold_kernel(in_ref, *refs):
    refs[-1][...] = in_ref[...]


def message_kernel(place_ref, keep_ref, mate_ref, extra_ref, *out_refs):
    zl, core = place_ref[1], place_ref[2]
    if len(out_refs) == 5:
        out_refs[4][...] = extra_ref[...]
    for k in range(4):
        target = lax.rem(zl + k, 4)
        out_refs[k][core] = keep_ref[target]
        out_refs[k][1 - core] = mate_ref[target]


def send_kernel(place_ref, in_ref, *out_refs):
    x = place_ref[3]
    for k in range(4):
        for block in range(4):
            out_refs[k][block * 64:(block + 1) * 64] = in_ref[block, 0:64]
        out_refs[k][256:336] = in_ref[lax.rem(x + k, 4), 64:144]


def weight_kernel(place_ref, *refs):
    y, zl = place_ref[0], place_ref[1]
    for piece, ky in enumerate((0, 1, -1, 2)):
        from_y = lax.rem(y - ky + 4, 4)
        for kz in range(4):
            from_zl = lax.rem(zl - kz + 4, 4)
            row = (from_zl // 2) * HALF + from_y * HW + lax.rem(from_zl, 2) * 96
            refs[-1][pl.ds(pl.multiple_of(row, 32), 96), :] = refs[piece][kz]


def attention_kernel(first, place_ref, *refs):
    blocks, refs = refs[:8], refs[8:]
    if first:
        w_ref, out_ref, keep_ref, k01, v01, k2, v2, q01, q2 = refs
    else:
        w_ref, text_ref, out_ref, k01, v01, k2, v2, q01, q2 = refs
    core, x = place_ref[2], place_ref[3]
    if first:
        rows = jnp.concatenate([
            jnp.concatenate([blocks[k + e * 4][n * 64:(n + 1) * 64] for n in range(4)], axis=1)
            for k in range(4) for e in range(2)
        ], axis=0)
        for which in range(2):
            span = slice(256 + which * 40, 256 + (which + 1) * 40)
            text = jnp.concatenate([b[span].astype(f32) for b in blocks], axis=0)
            keep_ref[which] = jnp.where(core == 0, text[:, :HW], text[:, HW:]).astype(bf16)
        text_ref = keep_ref
        qkv = jnp.dot(rows, w_ref[...], preferred_element_type=f32)
    else:
        mine = jnp.concatenate([b[...] for b in blocks[:4]], axis=0)
        other = jnp.concatenate([b[...] for b in blocks[4:]], axis=0)
        w_mine = w_ref[pl.ds(pl.multiple_of(core * HALF, HALF), HALF), :]
        w_other = w_ref[pl.ds(pl.multiple_of((1 - core) * HALF, HALF), HALF), :]
        qkv = jnp.dot(mine, w_mine, preferred_element_type=f32)
        qkv = qkv + jnp.dot(other, w_other, preferred_element_type=f32)
    scale = HEAD_DIM ** (-0.5)
    q01[...] = (qkv[:, 0:128] * scale).astype(bf16)
    k01[0:TOK, :] = qkv[:, 128:256].astype(bf16)
    v01[0:TOK, :] = qkv[:, 256:384].astype(bf16)
    q2[...] = (qkv[:, 384:448] * scale).astype(bf16)
    k2[0:TOK, :] = qkv[:, 448:512].astype(bf16)
    v2[0:TOK, :] = qkv[:, 512:576].astype(bf16)
    k01[TOK:, :] = text_ref[0, :, 0:128]
    v01[TOK:, :] = text_ref[1, :, 0:128]
    k2[TOK:, :] = text_ref[0, :, 128:192]
    v2[TOK:, :] = text_ref[1, :, 128:192]
    lane = lax.broadcasted_iota(jnp.int32, (TOK, 128), 1)

    def attend(query, keys, values):
        scores = lax.dot_general(
            query, keys, (((1,), (1,)), ((), ())), preferred_element_type=f32
        )
        top = jnp.max(scores, axis=-1, keepdims=True)
        exp_scores = jnp.exp(scores - top)
        total = jnp.sum(exp_scores, axis=-1, keepdims=True)
        weights = (exp_scores * (1.0 / total)).astype(bf16)
        return jnp.dot(weights, values, preferred_element_type=f32)

    pair = q01[...]
    zero = jnp.zeros_like(pair)
    out0 = attend(jnp.where(lane < 64, pair, zero), k01[...], v01[...])
    out1 = attend(jnp.where(lane < 64, zero, pair), k01[...], v01[...])
    out01 = jnp.where(lane < 64, out0, out1).astype(bf16)
    out2 = attend(q2[...], k2[...], v2[...])
    for part in range(TOK // 16):
        slot, place = part // 8, part % 8
        if first:
            sub, zh = place % 4, (core if place < 4 else 1 - core)
        else:
            sub, zh = place // 2, place % 2
        target = (sub * 4 + lax.rem(x - slot + 4, 4)) * 2 + zh
        start = part * 16
        out_ref[target, 0:16] = out01[start:start + 16]
        out_ref[target, 16:24] = jnp.concatenate(
            [out2[start:start + 8], out2[start + 8:start + 16]], axis=1
        ).astype(bf16)


def terms_kernel(first, place_ref, att_ref, *refs):
    if first:
        messages, (part_ref, total_ref, mod_ref) = refs[:4], refs[4:]
        for k in range(4):
            from_zl = lax.rem(place_ref[1] - k + 4, 4)
            for core in range(2):
                mod_ref[from_zl * 2 + core] = messages[k][core]
        lat_ref = mod_ref
    else:
        lat_ref, mod_ref, part_ref, total_ref = refs
    run = jnp.where(place_ref[0] == 0, lat_ref[0, 0:16], 0.0)
    for j in range(8):
        part_ref[j] = run
        sub, zh = j // 2, j % 2
        pieces = []
        for k in range(4):
            piece = att_ref[(sub * 4 + k) * 2 + zh].astype(f32)
            tail = jnp.concatenate([piece[16:24, 0:64], piece[16:24, 64:128]], axis=0)
            pieces += [piece[0:16], tail]
        attended = jnp.concatenate(pieces, axis=1)
        run = run + mod_ref[j, 19:20] * (lat_ref[j, 0:16] + mod_ref[j, 18:19] * attended)
    for k in range(4):
        total_ref[k] = run


def later_offset(place_ref, totals_ref):
    offset = jnp.zeros((16, HALF), f32)
    for k in range(3):
        offset = offset + jnp.where(k < place_ref[0], totals_ref[k], 0.0)
    return offset


def final_kernel(place_ref, part_ref, lat_ref, totals_ref, chg_ref, keep_ref, mate_ref):
    offset = later_offset(place_ref, totals_ref)
    core = place_ref[2]
    for j in range(8):
        new = part_ref[j] + offset
        chg_ref[j:j + 1, :] = jnp.full((1, 128), jnp.max(jnp.abs(new - lat_ref[j])), f32)
        for ref, wanted in ((keep_ref, core), (mate_ref, 1 - core)):
            @pl.when(wanted == j % 2)
            def _(ref=ref, new=new, j=j):
                ref[j // 2] = new


def update_kernel(place_ref, part_ref, lat_ref, totals_ref, new_ref, chg_ref, stats_ref):
    offset = later_offset(place_ref, totals_ref)
    lane = lax.broadcasted_iota(jnp.int32, (16, 128), 1)
    for j in range(8):
        new = part_ref[j] + offset
        new_ref[j] = new
        change = jnp.max(jnp.abs(new - lat_ref[j, 0:16]))
        chg_ref[j:j + 1, :] = jnp.full((1, 128), change, f32)
        average = jnp.mean(new, axis=-1, keepdims=True)
        centred = new - average
        spread = jnp.sum(centred * centred, axis=-1, keepdims=True)
        stats_ref[j] = jnp.where(lane == 0, average, spread)


def modulate_kernel(new_ref, mine_ref, other_ref, mod_ref, out_ref):
    for j in range(8):
        mean_a, mean_b = mine_ref[j][:, 0:1], other_ref[j][:, 0:1]
        spread = mine_ref[j][:, 1:2] + other_ref[j][:, 1:2]
        average = (mean_a + mean_b) * 0.5
        gap = mean_a - mean_b
        variance = (spread + gap * gap * (HALF * 0.5)) * (1.0 / D)
        normed = (new_ref[j] - average) * lax.rsqrt(variance + 1e-06)
        out_ref[j] = (
            normed * (1.0 + mod_ref[j, 17:18]) + mod_ref[j, 16:17]
        ).astype(bf16)


def place_kernel(place_ref, *refs):
    out_ref = refs[4]
    for k in range(4):
        row = pl.multiple_of(lax.rem(place_ref[1] - k + 4, 4) * 16, 16)
        for x in range(4):
            cols = slice(x * HW, (x + 1) * HW)
            out_ref[pl.ds(row, 16), x * 2 * HW:(x + 1) * 2 * HW] = jnp.concatenate(
                [refs[k][0][:, cols], refs[k][1][:, cols]], axis=1
            )


def on_device(states, qkv_weight, text_kv, mod_table, step_table, step_ids):
    y, zl, c, x, zh = (lax.axis_index(name) for name in AXES)
    same = c == zh
    place = jnp.stack([y, zl, c, x]).astype(jnp.int32)

    with jax.named_scope("weights"):
        w = call(columns_kernel, struct(48, 3 * HW, dtype=bf16), 1, 0)(
            jnp.transpose(qkv_weight, (1, 0, 2))
        )
        w_b = [permute(w, ("c", "zh"), lambda p, k=k: {"c": p["zh"], "zh": 1 - p["zh"]}
                       if p["c"] == k else None) for k in range(2)]
        w_a = permute(w, ("c", "zh"), lambda p: None if p["c"] == p["zh"] else
                      {"c": 1 - p["c"], "zh": p["zh"]})
        w0 = jnp.where(same, jnp.where(c == 0, w, w_a), w_b[0])
        w1 = jnp.where(same, jnp.where(c == 1, w, w_a), w_b[1])
        w2 = jnp.concatenate([w0, w1], axis=0)
        w8 = jnp.stack([w2, shift_z(w2, 1), shift_z(w2, 2), shift_z(w2, -1)])

    with jax.named_scope("start"):
        mod_own = lax.dynamic_index_in_dim(mod_table, step_ids[0], 0, keepdims=False)
        packed, keep, mate = call(
            start_kernel,
            (struct(4, 144, BLOCK, dtype=bf16), struct(4, 24, HALF), struct(4, 24, HALF)),
            3, 3,
        )(place, step_ids, step_table, states, mod_own, text_kv)
    with jax.named_scope("gather_first"):
        packed = call(hold_kernel, struct(4, 144, BLOCK, dtype=bf16), 1, 0, after=1)(packed, w8)
        packed = swap_core_zh(packed, same)
        sends = call(send_kernel, (struct(336, BLOCK, dtype=bf16),) * 4, 1, 1)(place, packed)
        mine = [sends[0]] + [shift(sends[k], "x", k) for k in (1, 2, 3)]
        blocks = mine + [shift(b, "c", 1) for b in mine]

    with jax.named_scope("weights_y"):
        pieces = [w8, shift(w8, "y", 1), shift(w8, "y", -1)]
        pieces.append(shift(pieces[1], "y", 1))

    with jax.named_scope("states"):
        messages = call(message_kernel, (struct(2, 24, HALF),) * 4, 2, 1, after=1)(
            place, keep, shift(mate, "c", 1), pieces[1]
        )
        messages = [messages[0]] + [shift(messages[k], "zl", k) for k in (1, 2, 3)]

    with jax.named_scope("weights_y"):
        weight = call(weight_kernel, struct(D, 3 * HW, dtype=bf16), 4, 1, after=3)(
            place, *pieces, *messages[1:]
        )

    text = None
    for sweep in range(SWEEPS):
        last = sweep == SWEEPS - 1
        with jax.named_scope("attention"):
            outs = (struct(32, 24, 128, dtype=bf16),)
            scratch = [
                pltpu.VMEM((KEYS, 128), bf16), pltpu.VMEM((KEYS, 128), bf16),
                pltpu.VMEM((KEYS, 64), bf16), pltpu.VMEM((KEYS, 64), bf16),
                pltpu.VMEM((TOK, 128), bf16), pltpu.VMEM((TOK, 64), bf16),
            ]
            if sweep == 0:
                operands = (*blocks, weight)
                outs = outs + (struct(2, TXT, HW, dtype=bf16),)
            else:
                operands = (*blocks, weight, text)
            spaces = [pltpu.SMEM] + [pltpu.VMEM] * len(operands)
            attended, *text_out = pl.pallas_call(
                functools.partial(attention_kernel, sweep == 0),
                out_shape=outs,
                in_specs=[pl.BlockSpec(memory_space=space) for space in spaces],
                out_specs=tuple(pl.BlockSpec(memory_space=pltpu.VMEM) for _ in outs),
                compiler_params=pltpu.CompilerParams(vmem_limit_bytes=24 * MIB),
                cost_estimate=pl.CostEstimate(
                    flops=2 * TOK * D * 3 * HW + 4 * TOK * KEYS * HW,
                    bytes_accessed=24 << 20, transcendentals=3 * TOK * KEYS,
                ),
                scratch_shapes=scratch,
            )(place, *operands)
            text = text_out[0] if text_out else text
        with jax.named_scope("to_prefix"):
            attended = lax.all_to_all(attended, ("zl", "x", "zh"), 0, 0)
        with jax.named_scope("prefix"):
            outs = (struct(8, 16, HALF), struct(4, 16, HALF))
            if sweep == 0:
                part, total, mods = call(
                    functools.partial(terms_kernel, True), outs + (struct(8, 24, HALF),), 5, 1
                )(place, attended, *messages)
                lat = mods
            else:
                part, total = call(functools.partial(terms_kernel, False), outs, 3, 1)(
                    place, attended, lat, mods
                )
            totals = lax.all_to_all(total, "y", 0, 0)
            if last:
                break
            lat, change, stats = call(
                update_kernel, (struct(8, 16, HALF), struct(8, 128), struct(8, 16, 128)), 3, 1
            )(place, part, lat, totals)
        if not last:
            with jax.named_scope("norm"):
                modulated = call(
                    modulate_kernel, struct(8, 16, HALF, dtype=bf16), 4, 0
                )(lat, stats, shift(stats, "c", 1), mods)
            with jax.named_scope("gather"):
                modulated = lax.all_to_all(modulated, ("zl", "zh"), 0, 0).reshape(128, HALF)
                mine = [modulated] + [shift(modulated, "x", k) for k in (1, 2, 3)]
                blocks = mine + [shift(b, "c", 1) for b in mine]
    with jax.named_scope("place"):
        top, keep, mate = call(
            final_kernel, (struct(8, 128), struct(4, 16, HALF), struct(4, 16, HALF)), 3, 1
        )(place, part, lat, totals)
        top = jnp.concatenate([change, top], axis=0)
        top = jnp.maximum(top, shift(top, "c", 1))
        *outs, top = call(
            message_kernel, (struct(2, 16, HALF),) * 4 + (struct(16, 128),), 3, 1
        )(place, keep, shift(mate, "c", 1), top)
        outs = [outs[0]] + [shift(outs[k], "zl", k) for k in (1, 2, 3)]
        out = call(place_kernel, struct(ROWS, D), 4, 1)(place, *outs)
    with jax.named_scope("changes"):
        top = functools.reduce(jnp.maximum, [top] + [shift(top, "zl", k) for k in (1, 2, 3)])
        top = functools.reduce(jnp.maximum, [top] + [shift(top, "x", k) for k in (1, 2, 3)])
        top = jnp.maximum(top, shift(top, "zh", 1))
        top = top[:, 0].reshape(SWEEPS, 8)
        top = lax.dynamic_slice_in_dim(top, zl * 2 + c, 1, axis=1)
    return out[None], top


def solution(mesh):
    fine = Mesh(mesh.devices.reshape([SIZES[name] for name in AXES]), AXES)
    tm, seq = ("y", "zl", "c"), ("x", "zh")
    in_specs = (
        P(tm, seq, None), P(tm, None, seq), P(tm, seq, None, None), P(), P(), P(tm),
    )
    out_specs = (P(tm, seq, None), P(None, tm))
    return jax.shard_map(
        on_device, mesh=fine, in_specs=in_specs, out_specs=out_specs, check_vma=False
    )
```

```python
import functools
import itertools

import jax
import jax.numpy as jnp
from jax import lax
from jax.experimental import pallas as pl
from jax.experimental.pallas import tpu as pltpu
from jax.sharding import Mesh, PartitionSpec as P

AXES = ("y", "zl", "c", "x", "zh")
SIZES = {"y": 4, "zl": 4, "c": 2, "x": 4, "zh": 2}

HEAD_DIM = 64
SWEEPS = 2
D = 1536
HALF = 768
BLOCK = 384
HW = 192
ROWS = 64
TOK = 512
TXT = 320
KEYS = TOK + TXT
MIB = 1024 * 1024
f32, bf16 = jnp.float32, jnp.bfloat16


def permute(value, axes, move):
    def index(place):
        flat = 0
        for name in axes:
            flat = flat * SIZES[name] + place[name] % SIZES[name]
        return flat

    pairs = []
    for coords in itertools.product(*[range(SIZES[name]) for name in axes]):
        place = dict(zip(axes, coords))
        target = move(dict(place))
        if target is not None:
            pairs.append((index(place), index(target)))
    return lax.ppermute(value, axes if len(axes) > 1 else axes[0], pairs)


def shift(value, axis, amount):
    return permute(value, (axis,), lambda p: {axis: p[axis] + amount})


def shift_z(value, amount):
    def move(p):
        ring = (p["zh"] * 4 + p["zl"] + amount) % 8
        return {"zl": ring % 4, "zh": ring // 4}

    return permute(value, ("zl", "zh"), move)


def swap_core_zh(value, same):
    moved = permute(
        value, ("c", "zh"),
        lambda p: None if p["c"] == p["zh"] else {"c": p["zh"], "zh": p["c"]},
    )
    return jnp.where(same, value, moved)


def call(kernel, out_shape, n_vmem, n_smem, limit=6, after=0):
    return pl.pallas_call(
        kernel,
        out_shape=out_shape,
        in_specs=[pl.BlockSpec(memory_space=pltpu.SMEM)] * n_smem
        + [pl.BlockSpec(memory_space=pltpu.VMEM)] * n_vmem
        + [pl.BlockSpec(memory_space=pl.ANY)] * after,
        out_specs=jax.tree.map(lambda _: pl.BlockSpec(memory_space=pltpu.VMEM), out_shape),
        compiler_params=pltpu.CompilerParams(vmem_limit_bytes=limit * MIB),
    )


def struct(*shape, dtype=f32):
    return jax.ShapeDtypeStruct(shape, dtype)


def half_columns(half):
    return [slice(k * 2 * HW + half * HW, k * 2 * HW + (half + 1) * HW) for k in range(4)]


def columns_kernel(w_ref, out_ref):
    parts = [w_ref[k, :, :128] for k in range(3)] + [w_ref[k, :, 128:] for k in range(3)]
    out_ref[...] = jnp.concatenate(parts, axis=1)


def start_kernel(place_ref, ids_ref, steps_ref, lat_ref, mod_ref, text_ref,
                 out_ref, keep_ref, mate_ref):
    latent = lat_ref[0]
    average = jnp.mean(latent, axis=-1, keepdims=True)
    centred = latent - average
    variance = jnp.mean(centred * centred, axis=-1, keepdims=True)
    normed = centred * lax.rsqrt(variance + 1e-06)
    modulated = (normed * (1.0 + mod_ref[1:2, :]) + mod_ref[0:1, :]).astype(bf16)
    raw = text_ref[0].astype(f32)
    rows = jnp.concatenate([raw[:, 0, :], raw[:, 1, :]], axis=0).astype(bf16)
    step = jnp.full((5, HALF), -steps_ref[ids_ref[0]], f32)
    for half in range(2):
        piece = jnp.concatenate([modulated[:, s] for s in half_columns(half)], axis=1)
        out_ref[half * 2, 0:64] = piece[:, 0:BLOCK]
        out_ref[half * 2 + 1, 0:64] = piece[:, BLOCK:]
        piece = jnp.concatenate([latent[:, s] for s in half_columns(half)], axis=1)
        mods = jnp.concatenate([mod_ref[:, s] for s in half_columns(half)], axis=1)
        below = jnp.concatenate([mods, step], axis=0)
        for ref, wanted in ((keep_ref, place_ref[2]), (mate_ref, 1 - place_ref[2])):
            @pl.when(wanted == half)
            def _(ref=ref, piece=piece, below=below):
                for sub in range(4):
                    ref[sub, 0:16] = piece[sub * 16:(sub + 1) * 16]
                    ref[sub, 16:24] = below
    for k in range(4):
        out_ref[k, 64:144] = rows[:, k * BLOCK:(k + 1) * BLOCK]


def hold_kernel(in_ref, *refs):
    refs[-1][...] = in_ref[...]


def message_kernel(place_ref, keep_ref, mate_ref, extra_ref, *out_refs):
    zl, core = place_ref[1], place_ref[2]
    if len(out_refs) == 5:
        out_refs[4][...] = extra_ref[...]
    for k in range(4):
        target = lax.rem(zl + k, 4)
        out_refs[k][core] = keep_ref[target]
        out_refs[k][1 - core] = mate_ref[target]


def send_kernel(place_ref, in_ref, *out_refs):
    x = place_ref[3]
    for k in range(4):
        for block in range(4):
            out_refs[k][block * 64:(block + 1) * 64] = in_ref[block, 0:64]
        out_refs[k][256:336] = in_ref[lax.rem(x + k, 4), 64:144]


def weight_kernel(place_ref, *refs):
    y, zl = place_ref[0], place_ref[1]
    for piece, ky in enumerate((0, 1, -1, 2)):
        from_y = lax.rem(y - ky + 4, 4)
        for kz in range(4):
            from_zl = lax.rem(zl - kz + 4, 4)
            row = (from_zl // 2) * HALF + from_y * HW + lax.rem(from_zl, 2) * 96
            refs[-1][pl.ds(pl.multiple_of(row, 32), 96), :] = refs[piece][kz]


def attention_kernel(first, place_ref, *refs):
    blocks, refs = refs[:8], refs[8:]
    if first:
        w_ref, out_ref, keep_ref, k01, v01, k2, v2, q01, q2 = refs
    else:
        w_ref, text_ref, out_ref, k01, v01, k2, v2, q01, q2 = refs
    core, x = place_ref[2], place_ref[3]
    if first:
        rows = jnp.concatenate([
            jnp.concatenate([blocks[k + e * 4][n * 64:(n + 1) * 64] for n in range(4)], axis=1)
            for k in range(4) for e in range(2)
        ], axis=0)
        for which in range(2):
            span = slice(256 + which * 40, 256 + (which + 1) * 40)
            text = jnp.concatenate([b[span].astype(f32) for b in blocks], axis=0)
            keep_ref[which] = jnp.where(core == 0, text[:, :HW], text[:, HW:]).astype(bf16)
        text_ref = keep_ref
        qkv = jnp.dot(rows, w_ref[...], preferred_element_type=f32)
    else:
        mine = jnp.concatenate([b[...] for b in blocks[:4]], axis=0)
        other = jnp.concatenate([b[...] for b in blocks[4:]], axis=0)
        w_mine = w_ref[pl.ds(pl.multiple_of(core * HALF, HALF), HALF), :]
        w_other = w_ref[pl.ds(pl.multiple_of((1 - core) * HALF, HALF), HALF), :]
        qkv = jnp.dot(mine, w_mine, preferred_element_type=f32)
        qkv = qkv + jnp.dot(other, w_other, preferred_element_type=f32)
    scale = HEAD_DIM ** (-0.5)
    q01[...] = (qkv[:, 0:128] * scale).astype(bf16)
    k01[0:TOK, :] = qkv[:, 128:256].astype(bf16)
    v01[0:TOK, :] = qkv[:, 256:384].astype(bf16)
    q2[...] = (qkv[:, 384:448] * scale).astype(bf16)
    k2[0:TOK, :] = qkv[:, 448:512].astype(bf16)
    v2[0:TOK, :] = qkv[:, 512:576].astype(bf16)
    k01[TOK:, :] = text_ref[0, :, 0:128]
    v01[TOK:, :] = text_ref[1, :, 0:128]
    k2[TOK:, :] = text_ref[0, :, 128:192]
    v2[TOK:, :] = text_ref[1, :, 128:192]
    lane = lax.broadcasted_iota(jnp.int32, (TOK, 128), 1)

    def attend(query, keys, values):
        scores = lax.dot_general(
            query, keys, (((1,), (1,)), ((), ())), preferred_element_type=f32
        )
        top = jnp.max(scores, axis=-1, keepdims=True)
        exp_scores = jnp.exp(scores - top)
        total = jnp.sum(exp_scores, axis=-1, keepdims=True)
        weights = (exp_scores * (1.0 / total)).astype(bf16)
        return jnp.dot(weights, values, preferred_element_type=f32)

    pair = q01[...]
    zero = jnp.zeros_like(pair)
    out0 = attend(jnp.where(lane < 64, pair, zero), k01[...], v01[...])
    out1 = attend(jnp.where(lane < 64, zero, pair), k01[...], v01[...])
    out01 = jnp.where(lane < 64, out0, out1).astype(bf16)
    out2 = attend(q2[...], k2[...], v2[...])
    for part in range(TOK // 16):
        slot, place = part // 8, part % 8
        if first:
            sub, zh = place % 4, (core if place < 4 else 1 - core)
        else:
            sub, zh = place // 2, place % 2
        target = (sub * 4 + lax.rem(x - slot + 4, 4)) * 2 + zh
        start = part * 16
        out_ref[target, 0:16] = out01[start:start + 16]
        out_ref[target, 16:24] = jnp.concatenate(
            [out2[start:start + 8], out2[start + 8:start + 16]], axis=1
        ).astype(bf16)


def terms_kernel(first, place_ref, att_ref, *refs):
    if first:
        messages, (part_ref, total_ref, mod_ref) = refs[:4], refs[4:]
        for k in range(4):
            from_zl = lax.rem(place_ref[1] - k + 4, 4)
            for core in range(2):
                mod_ref[from_zl * 2 + core] = messages[k][core]
        lat_ref = mod_ref
    else:
        lat_ref, mod_ref, part_ref, total_ref = refs
    run = jnp.where(place_ref[0] == 0, lat_ref[0, 0:16], 0.0)
    for j in range(8):
        part_ref[j] = run
        sub, zh = j // 2, j % 2
        pieces = []
        for k in range(4):
            piece = att_ref[(sub * 4 + k) * 2 + zh].astype(f32)
            tail = jnp.concatenate([piece[16:24, 0:64], piece[16:24, 64:128]], axis=0)
            pieces += [piece[0:16], tail]
        attended = jnp.concatenate(pieces, axis=1)
        run = run + mod_ref[j, 19:20] * (lat_ref[j, 0:16] + mod_ref[j, 18:19] * attended)
    for k in range(4):
        total_ref[k] = run


def later_offset(place_ref, totals_ref):
    offset = jnp.zeros((16, HALF), f32)
    for k in range(3):
        offset = offset + jnp.where(k < place_ref[0], totals_ref[k], 0.0)
    return offset


def final_kernel(place_ref, part_ref, lat_ref, totals_ref, chg_ref, keep_ref, mate_ref):
    offset = later_offset(place_ref, totals_ref)
    core = place_ref[2]
    for j in range(8):
        new = part_ref[j] + offset
        chg_ref[j:j + 1, :] = jnp.full((1, 128), jnp.max(jnp.abs(new - lat_ref[j])), f32)
        for ref, wanted in ((keep_ref, core), (mate_ref, 1 - core)):
            @pl.when(wanted == j % 2)
            def _(ref=ref, new=new, j=j):
                ref[j // 2] = new


def update_kernel(place_ref, part_ref, lat_ref, totals_ref, new_ref, chg_ref, stats_ref):
    offset = later_offset(place_ref, totals_ref)
    lane = lax.broadcasted_iota(jnp.int32, (16, 128), 1)
    for j in range(8):
        new = part_ref[j] + offset
        new_ref[j] = new
        change = jnp.max(jnp.abs(new - lat_ref[j, 0:16]))
        chg_ref[j:j + 1, :] = jnp.full((1, 128), change, f32)
        average = jnp.mean(new, axis=-1, keepdims=True)
        centred = new - average
        spread = jnp.sum(centred * centred, axis=-1, keepdims=True)
        stats_ref[j] = jnp.where(lane == 0, average, spread)


def modulate_kernel(new_ref, mine_ref, other_ref, mod_ref, out_ref):
    for j in range(8):
        mean_a, mean_b = mine_ref[j][:, 0:1], other_ref[j][:, 0:1]
        spread = mine_ref[j][:, 1:2] + other_ref[j][:, 1:2]
        average = (mean_a + mean_b) * 0.5
        gap = mean_a - mean_b
        variance = (spread + gap * gap * (HALF * 0.5)) * (1.0 / D)
        normed = (new_ref[j] - average) * lax.rsqrt(variance + 1e-06)
        out_ref[j] = (
            normed * (1.0 + mod_ref[j, 17:18]) + mod_ref[j, 16:17]
        ).astype(bf16)


def place_kernel(place_ref, *refs):
    out_ref = refs[4]
    for k in range(4):
        row = pl.multiple_of(lax.rem(place_ref[1] - k + 4, 4) * 16, 16)
        for x in range(4):
            cols = slice(x * HW, (x + 1) * HW)
            out_ref[pl.ds(row, 16), x * 2 * HW:(x + 1) * 2 * HW] = jnp.concatenate(
                [refs[k][0][:, cols], refs[k][1][:, cols]], axis=1
            )


def on_device(states, qkv_weight, text_kv, mod_table, step_table, step_ids):
    y, zl, c, x, zh = (lax.axis_index(name) for name in AXES)
    same = c == zh
    place = jnp.stack([y, zl, c, x]).astype(jnp.int32)

    with jax.named_scope("weights"):
        w = call(columns_kernel, struct(48, 3 * HW, dtype=bf16), 1, 0)(
            jnp.transpose(qkv_weight, (1, 0, 2))
        )
        w_b = [permute(w, ("c", "zh"), lambda p, k=k: {"c": p["zh"], "zh": 1 - p["zh"]}
                       if p["c"] == k else None) for k in range(2)]
        w_a = permute(w, ("c", "zh"), lambda p: None if p["c"] == p["zh"] else
                      {"c": 1 - p["c"], "zh": p["zh"]})
        w0 = jnp.where(same, jnp.where(c == 0, w, w_a), w_b[0])
        w1 = jnp.where(same, jnp.where(c == 1, w, w_a), w_b[1])
        w2 = jnp.concatenate([w0, w1], axis=0)
        w_far = jnp.concatenate([shift_z(w0, 2), shift_z(w1, -2)], axis=0)
        w8 = jnp.stack([w2, shift_z(w2, 1), w_far, shift_z(w2, -1)])

    with jax.named_scope("start"):
        mod_own = lax.dynamic_index_in_dim(mod_table, step_ids[0], 0, keepdims=False)
        packed, keep, mate = call(
            start_kernel,
            (struct(4, 144, BLOCK, dtype=bf16), struct(4, 24, HALF), struct(4, 24, HALF)),
            3, 3,
        )(place, step_ids, step_table, states, mod_own, text_kv)
    with jax.named_scope("gather_first"):
        packed = call(hold_kernel, struct(4, 144, BLOCK, dtype=bf16), 1, 0, after=1)(packed, w8)
        packed = swap_core_zh(packed, same)
        sends = call(send_kernel, (struct(336, BLOCK, dtype=bf16),) * 4, 1, 1)(place, packed)
        mine = [sends[0]] + [shift(sends[k], "x", k) for k in (1, 2, 3)]
        blocks = mine + [shift(b, "c", 1) for b in mine]

    with jax.named_scope("weights_y"):
        pieces = [w8, shift(w8, "y", 1), shift(w8, "y", -1)]
        pieces.append(shift(pieces[1], "y", 1))

    with jax.named_scope("states"):
        messages = call(message_kernel, (struct(2, 24, HALF),) * 4, 2, 1, after=1)(
            place, keep, shift(mate, "c", 1), pieces[1]
        )
        messages = [messages[0]] + [shift(messages[k], "zl", k) for k in (1, 2, 3)]

    with jax.named_scope("weights_y"):
        weight = call(weight_kernel, struct(D, 3 * HW, dtype=bf16), 4, 1, after=3)(
            place, *pieces, *messages[1:]
        )

    text = None
    for sweep in range(SWEEPS):
        last = sweep == SWEEPS - 1
        with jax.named_scope("attention"):
            outs = (struct(32, 24, 128, dtype=bf16),)
            scratch = [
                pltpu.VMEM((KEYS, 128), bf16), pltpu.VMEM((KEYS, 128), bf16),
                pltpu.VMEM((KEYS, 64), bf16), pltpu.VMEM((KEYS, 64), bf16),
                pltpu.VMEM((TOK, 128), bf16), pltpu.VMEM((TOK, 64), bf16),
            ]
            if sweep == 0:
                operands = (*blocks, weight)
                outs = outs + (struct(2, TXT, HW, dtype=bf16),)
            else:
                operands = (*blocks, weight, text)
            spaces = [pltpu.SMEM] + [pltpu.VMEM] * len(operands)
            attended, *text_out = pl.pallas_call(
                functools.partial(attention_kernel, sweep == 0),
                out_shape=outs,
                in_specs=[pl.BlockSpec(memory_space=space) for space in spaces],
                out_specs=tuple(pl.BlockSpec(memory_space=pltpu.VMEM) for _ in outs),
                compiler_params=pltpu.CompilerParams(vmem_limit_bytes=24 * MIB),
                cost_estimate=pl.CostEstimate(
                    flops=2 * TOK * D * 3 * HW + 4 * TOK * KEYS * HW,
                    bytes_accessed=24 << 20, transcendentals=3 * TOK * KEYS,
                ),
                scratch_shapes=scratch,
            )(place, *operands)
            text = text_out[0] if text_out else text
        with jax.named_scope("to_prefix"):
            attended = lax.all_to_all(attended, ("zl", "x", "zh"), 0, 0)
        with jax.named_scope("prefix"):
            outs = (struct(8, 16, HALF), struct(4, 16, HALF))
            if sweep == 0:
                part, total, mods = call(
                    functools.partial(terms_kernel, True), outs + (struct(8, 24, HALF),), 5, 1
                )(place, attended, *messages)
                lat = mods
            else:
                part, total = call(functools.partial(terms_kernel, False), outs, 3, 1)(
                    place, attended, lat, mods
                )
            totals = lax.all_to_all(total, "y", 0, 0)
            if last:
                break
            lat, change, stats = call(
                update_kernel, (struct(8, 16, HALF), struct(8, 128), struct(8, 16, 128)), 3, 1
            )(place, part, lat, totals)
        if not last:
            with jax.named_scope("norm"):
                modulated = call(
                    modulate_kernel, struct(8, 16, HALF, dtype=bf16), 4, 0
                )(lat, stats, shift(stats, "c", 1), mods)
            with jax.named_scope("gather"):
                modulated = lax.all_to_all(modulated, ("zl", "zh"), 0, 0).reshape(128, HALF)
                mine = [modulated] + [shift(modulated, "x", k) for k in (1, 2, 3)]
                blocks = mine + [shift(b, "c", 1) for b in mine]
    with jax.named_scope("place"):
        top, keep, mate = call(
            final_kernel, (struct(8, 128), struct(4, 16, HALF), struct(4, 16, HALF)), 3, 1
        )(place, part, lat, totals)
        top = jnp.concatenate([change, top], axis=0)
        top = jnp.maximum(top, shift(top, "c", 1))
        *outs, top = call(
            message_kernel, (struct(2, 16, HALF),) * 4 + (struct(16, 128),), 3, 1
        )(place, keep, shift(mate, "c", 1), top)
        outs = [outs[0]] + [shift(outs[k], "zl", k) for k in (1, 2, 3)]
        out = call(place_kernel, struct(ROWS, D), 4, 1)(place, *outs)
    with jax.named_scope("changes"):
        top = functools.reduce(jnp.maximum, [top] + [shift(top, "zl", k) for k in (1, 2, 3)])
        top = functools.reduce(jnp.maximum, [top] + [shift(top, "x", k) for k in (1, 2, 3)])
        top = jnp.maximum(top, shift(top, "zh", 1))
        top = top[:, 0].reshape(SWEEPS, 8)
        top = lax.dynamic_slice_in_dim(top, zl * 2 + c, 1, axis=1)
    return out[None], top


def solution(mesh):
    fine = Mesh(mesh.devices.reshape([SIZES[name] for name in AXES]), AXES)
    tm, seq = ("y", "zl", "c"), ("x", "zh")
    in_specs = (
        P(tm, seq, None), P(tm, None, seq), P(tm, seq, None, None), P(), P(), P(tm),
    )
    out_specs = (P(tm, seq, None), P(None, tm))
    return jax.shard_map(
        on_device, mesh=fine, in_specs=in_specs, out_specs=out_specs, check_vma=False
    )
```
